256 devices in a mesh: rep: 2 (over x_hi), ep: 128 (over y, z, x_lo, core).
Axes of the slice: x: 4 (x_hi: 2, x_lo: 2; x = x_hi * 2 + x_lo), y: 4, z: 8, core: 2. Of those that a mesh axis runs over, the one named last changes fastest.
Arguments:
- tokens: bfloat16 [2, 8192, 3584], P(None, ('rep', 'ep')), may hold values from -6 to 6
- routing: int32 [2, 8192, 8], P(None, ('rep', 'ep')), may hold values from 0 to 63, all different within a row; in each aligned block of 32 rows (0 to 31, 32 to 63, ..., all dimensions but the last counted through in order) at most 8 rows name the same one
- route_gate: float32 [2, 8192, 8], P(None, ('rep', 'ep')), may hold values from 0.05 to 0.5
- place_old: int32 [2, 64], replicated, may hold values from 0 to 63, as said below
- place_new: int32 [2, 64], replicated, may hold values from 0 to 63, as said below
- gate_proj: bfloat16 [2, 128, 3584, 512], P('rep', 'ep'), may hold values from -0.09375 to 0.09375
- up_proj: bfloat16 [2, 128, 3584, 512], P('rep', 'ep'), may hold values from -0.09375 to 0.09375
- down_proj: bfloat16 [2, 128, 512, 3584], P('rep', 'ep'), may hold values from -0.1875 to 0.1875
Outputs:
- combined: bfloat16 [2, 8192, 3584], P(None, ('rep', 'ep'))
The draws below stay inside these ranges and needn't reach their ends.
Inputs may be any that keep to these rules, and one draw needn't show every extreme that they name: `routing`: in the rows of one device of one batch (aligned blocks of 32 rows) no expert is named more than 8 times, a bound that some block reaches; a row names distinct experts. `place_old`: each row is a permutation of the experts. Each row is a permutation of the experts; at exactly 16 positions, the same in both rows, place_new[r, e] = place_old[1 - r, e] differs from place_old[r, e]; elsewhere it equals place_old.
All inputs are finite; a program needn't handle non-finite values.
Results may differ from the reference program's by a relative error of at most 0.0058.
Values may be sent and summed in bfloat16 or wider, within the bound.
A program may use at most 128 MiB of HBM per device.

```python
import math
import jax
import jax.numpy as jnp
import numpy as np
from jax import lax

D = 3584
FF = 1024
FF_DEV = 512
TOPK = 8
BATCHES = 2
TOK_DEV = 32
EXPERTS = 64
MOVES = 16
CAP = 8
TOKENS = 8192
N_REP = 2
N_EP = 128


def placement_pair(key):
    first_row = jax.random.permutation(jax.random.fold_in(key, 11), EXPERTS).astype(jnp.int32)
    shuffled = jax.random.permutation(jax.random.fold_in(key, 12), EXPERTS).astype(jnp.int32)
    lane_index = jnp.arange(EXPERTS, dtype=jnp.int32)
    inside = lane_index < MOVES
    following = jnp.where(inside, (lane_index + 1) % MOVES, MOVES + (lane_index - MOVES + 1) % (EXPERTS - MOVES))
    mapping = jnp.zeros((EXPERTS,), jnp.int32).at[shuffled].set(shuffled[following])
    second_row = first_row[mapping]
    is_moved = jnp.zeros((EXPERTS,), jnp.int32).at[shuffled].set(inside.astype(jnp.int32)) > 0
    old_layout = jnp.stack([first_row, second_row])
    new_layout = jnp.stack([jnp.where(is_moved, second_row, first_row), jnp.where(is_moved, first_row, second_row)])
    return (old_layout, new_layout)


def draw_place_old(key, part):
    return placement_pair(key)[0]


def draw_place_new(key, part):
    return placement_pair(key)[1]


def steps_of(key, extent, shards, smallest, top_value):
    factor_of, own = 1.0, jax.random.fold_in(key, 6)
    for axis_at, blocks in shards:
        heights = jnp.exp(jax.random.uniform(jax.random.fold_in(own, axis_at), (blocks,), jnp.float32, smallest / len(shards), top_value / len(shards)))
        factor_of = factor_of * jnp.repeat(heights, extent[axis_at] // blocks).reshape([-1 if axis == axis_at else 1 for axis in range(len(extent))])
    return factor_of


def routed_block(stream_key, own, number, rows, number_of, top, reach, lean):
    ranking = jax.random.permutation(stream_key, number_of)
    packed, usual = shares(number_of, rows * top, reach, lean, True), shares(number_of, rows * top, reach, lean, False)
    places = jnp.arange(number_of)

    def named(lengths, turn):
        used = int((lengths > 0).sum())
        fixed = max(1, used // 4)
        passed = fixed + (places - fixed + turn * (used - fixed)) % max(1, number_of - fixed)
        return jnp.zeros((number_of,), jnp.int32).at[ranking[jnp.where(places < fixed, places, passed)]].set(jnp.asarray(lengths, jnp.int32))

    lengths = jnp.where(number % 4 == 0, named(packed, number // 4), named(usual, number - number // 4 - 1))
    mixed = jax.random.permutation(jax.random.fold_in(own, 3), number_of)
    source_of, sink = mixed[0:number_of // 2 * 2:2], mixed[1:number_of // 2 * 2:2]
    margin = jnp.minimum(lengths[source_of] - 1, reach - lengths[sink]) // 2
    margin = jnp.where((source_of == ranking[0]) | (sink == ranking[0]) | (lengths[sink] == 0), 0, jnp.maximum(margin, 0))
    passed = jax.random.randint(jax.random.fold_in(own, 4), (number_of // 2,), 0, 1 << 20) % (margin + 1)
    lengths = lengths.at[source_of].add(-passed).at[sink].add(passed)
    items = jnp.searchsorted(jnp.cumsum(lengths), jnp.arange(rows * top), side="right").astype(jnp.int32)
    grid = items.reshape(top, rows).T
    grid = grid[jax.random.permutation(jax.random.fold_in(own, 1), rows)]
    turn = jax.random.randint(jax.random.fold_in(own, 2), (rows, 1), 0, top)
    return jnp.take_along_axis(grid, (jnp.arange(top)[None, :] + turn) % top, axis=1)


def shares(amount, total, bound, lean, full):
    loads = [(1 << 20) // math.isqrt(standing ** lean) + 1 for standing in range(1, amount + 1)]
    largest = bound if full else min(bound, max(-(-total // amount), total * loads[0] // sum(loads)))
    least = 1 if total - largest >= amount - 1 else 0
    holding, surplus = [largest] + [least] * (amount - 1), total - largest - least * (amount - 1)
    while surplus > 0:
        movable = [i for i in range(1, amount) if holding[i] < largest] or [i for i in range(1, amount) if holding[i] < bound]
        whole, remaining = sum([loads[i] for i in movable]), surplus
        for i in movable:
            extra = min(bound - holding[i], max(1, remaining * loads[i] // whole), surplus)
            holding[i] = holding[i] + extra
            surplus = surplus - extra
    return np.array(holding)


def noise(key, dims, deviation, limit, pieces=(), kind=jnp.bfloat16):
    result = deviation * jax.random.normal(key, dims, jnp.float32)
    if pieces:
        result = result * steps_of(key, dims, pieces, -0.22, 0.18)
    return jnp.clip(result, -limit, limit).astype(kind)


def setup_inputs(seed: int = 0) -> dict:
    seeds = jax.random.split(jax.random.key(seed), 9)
    tokens = noise(seeds[0], (BATCHES, TOKENS, D), 1.0, 6.0, ((1, 256),))
    routing_keys = jax.random.split(jax.random.fold_in(seeds[1], 1), BATCHES * TOKENS // TOK_DEV)
    routing_turns = jax.random.permutation(jax.random.fold_in(seeds[1], 3), BATCHES * TOKENS // TOK_DEV)
    routing = jax.vmap(lambda own, number: routed_block(jax.random.fold_in(seeds[1], 2), own, number, TOK_DEV, EXPERTS, TOPK, CAP, 2))(routing_keys, routing_turns).reshape((BATCHES, TOKENS, TOPK))
    route_gate = jnp.clip(jnp.exp(math.log(0.5) - 2.3025851 * jax.random.uniform(seeds[2], (BATCHES, TOKENS, TOPK), jnp.float32) ** steps_of(seeds[2], (BATCHES, TOKENS, TOPK), ((1, 256),), -0.2, 0.2)), 0.05, 0.5)
    place_old = draw_place_old(jax.random.fold_in(seeds[8], 71), 0)
    place_new = draw_place_new(jax.random.fold_in(seeds[8], 71), 0)
    gate_proj = noise(seeds[5], (N_REP, N_EP, D, FF_DEV), D ** -0.5, 0.09375, ((0, 2), (1, 128)))
    up_proj = noise(seeds[6], (N_REP, N_EP, D, FF_DEV), D ** -0.5, 0.09375, ((0, 2), (1, 128)))
    down_proj = noise(seeds[7], (N_REP, N_EP, FF_DEV, D), FF ** -0.5, 0.1875, ((0, 2), (1, 128)))
    return {"tokens": tokens, "routing": routing, "route_gate": route_gate, "place_old": place_old, "place_new": place_new, "gate_proj": gate_proj, "up_proj": up_proj, "down_proj": down_proj}


def expert_rows(row_block, gate_mat, up_mat, down_mat):
    gate_part = jnp.dot(row_block, gate_mat, preferred_element_type=jnp.float32)
    up_part = jnp.dot(row_block, up_mat, preferred_element_type=jnp.float32)
    hidden = (jax.nn.silu(gate_part) * up_part).astype(jnp.bfloat16)
    return jnp.dot(hidden, down_mat, preferred_element_type=jnp.float32).astype(jnp.bfloat16)


def reference(tokens, routing, route_gate, place_old, place_new, gate_proj, up_proj, down_proj):
    groups, positions = place_old.shape
    slot_count = groups * positions
    token_count = tokens.shape[1]
    row_bound = N_EP * CAP
    gate_flat = gate_proj.reshape(slot_count, 2, D, FF_DEV)
    up_flat = up_proj.reshape(slot_count, 2, D, FF_DEV)
    down_flat = down_proj.reshape(slot_count, 2, FF_DEV, D)
    group_of = (jnp.arange(token_count, dtype=jnp.int32) // (TOK_DEV * N_EP)).astype(jnp.int32)
    is_moved = (place_new != place_old).astype(jnp.int32)
    lane_index = jnp.arange(positions, dtype=jnp.int32)
    results = []
    for batch_at in range(BATCHES):
        layout = place_old if batch_at == 0 else place_new
        matches = layout[:, :, None] == lane_index[None, None, :]
        inverse = jnp.sum(jnp.where(matches, lane_index[None, :, None], 0), axis=1).astype(jnp.int32)
        position = inverse[group_of[:, None], routing[batch_at]]
        holder = jnp.broadcast_to(group_of[:, None], position.shape)
        if batch_at == 1:
            holder = jnp.bitwise_xor(holder, is_moved[holder, position])
        slot_index = (holder * positions + position).astype(jnp.int32)
        batch_tokens = tokens[batch_at]
        batch_gate = route_gate[batch_at]

        def visit_slot(accumulated, slot_now):
            is_hit = slot_index == slot_now
            weighting = jnp.sum(jnp.where(is_hit, batch_gate, 0.0), axis=1)
            is_used = jnp.any(is_hit, axis=1)
            row_index = jnp.nonzero(is_used, size=row_bound, fill_value=0)[0].astype(jnp.int32)
            is_live = jnp.arange(row_bound, dtype=jnp.int32) < jnp.sum(is_used.astype(jnp.int32))
            gathered = batch_tokens[row_index]
            first = expert_rows(gathered, gate_flat[slot_now, 0], up_flat[slot_now, 0], down_flat[slot_now, 0])
            second = expert_rows(gathered, gate_flat[slot_now, 1], up_flat[slot_now, 1], down_flat[slot_now, 1])
            produced = first.astype(jnp.float32) + second.astype(jnp.float32)
            factor = jnp.where(is_live, weighting[row_index], 0.0)
            accumulated = accumulated.at[row_index].add(factor[:, None] * produced)
            return accumulated, None

        accumulated, _ = lax.scan(visit_slot, jnp.zeros((token_count, D), jnp.float32), jnp.arange(slot_count, dtype=jnp.int32))
        results.append(accumulated.astype(jnp.bfloat16))
    return jnp.stack(results)
```

```python
import jax
import jax.numpy as jnp
from jax import lax
from jax.sharding import PartitionSpec as P

CAP = 8
BF16 = jnp.bfloat16
F32 = jnp.float32


def plan(experts, gates, chosen_by, layout, allowed):
    hit = (experts[:, :, None] == layout[None, None, :]) & allowed[chosen_by][:, None, :]
    named = jnp.any(hit, axis=1)
    weight = jnp.sum(jnp.where(hit, gates[:, :, None], 0.0), axis=1)
    tokens = experts.shape[0]
    before = jnp.tril(jnp.ones((tokens, tokens), BF16), -1)
    rank = jnp.dot(before, named.astype(BF16), preferred_element_type=F32).astype(jnp.int32)
    in_slot = named[:, :, None] & (rank[:, :, None] == jnp.arange(CAP, dtype=jnp.int32))
    positions = layout.shape[0]
    pick = in_slot.reshape(tokens, positions * CAP).astype(BF16)
    mix = jnp.where(in_slot, weight[:, :, None], 0.0).reshape(tokens, positions * CAP)
    return pick, mix


def ffn(rows, halves):
    total = None
    for gate_mat, up_mat, down_mat in halves:
        gate_part = jnp.dot(rows, gate_mat, preferred_element_type=F32)
        up_part = jnp.dot(rows, up_mat, preferred_element_type=F32)
        hidden = (jax.nn.silu(gate_part) * up_part).astype(BF16)
        part = jnp.dot(hidden, down_mat, preferred_element_type=F32)
        total = part if total is None else total + part
    return total.astype(BF16)


def body(tokens, routing, route_gate, place_old, place_new, gate_proj, up_proj, down_proj):
    ep_count = lax.axis_size("ep")
    positions = ep_count // 2
    rep = lax.axis_index("rep")
    batches, rows, width = tokens.shape
    groups = [[2 * e + c for e in range(positions)] for c in range(2)]
    swap_core = [(i, i ^ 1) for i in range(ep_count)]
    swap_rep = [(0, 1), (1, 0)]
    own = (gate_proj[0, 0], up_proj[0, 0], down_proj[0, 0])
    other = tuple(lax.ppermute(w, "ep", swap_core) for w in own)
    layout = lax.dynamic_index_in_dim(place_old, rep, 0, keepdims=False)
    moved = lax.dynamic_index_in_dim(place_new, rep, 0, keepdims=False) != layout

    their_tokens = lax.ppermute(tokens[1], "rep", swap_rep)
    their_routing = lax.ppermute(routing[1], "rep", swap_rep)
    their_gate = lax.ppermute(route_gate[1], "rep", swap_rep)

    mine = jnp.zeros((rows,), jnp.int32)
    anywhere = jnp.ones((1, positions), bool)
    plans = [
        plan(routing[0], route_gate[0], mine, layout, anywhere),
        plan(
            jnp.concatenate([routing[1], their_routing]),
            jnp.concatenate([route_gate[1], their_gate]),
            jnp.concatenate([mine, mine + 1]),
            layout,
            jnp.stack([~moved, moved]),
        ),
    ]
    sources = [tokens[0], jnp.concatenate([tokens[1], their_tokens])]

    def a2a(x):
        return lax.all_to_all(x, "ep", split_axis=0, concat_axis=0, axis_index_groups=groups, tiled=True)

    outs = []
    for (pick, mix), source in zip(plans, sources):
        packed = lax.dot_general(pick, source, (((0,), (0,)), ((), ())), preferred_element_type=F32).astype(BF16)
        received = a2a(packed.reshape(positions, CAP, width))
        produced = ffn(received.reshape(positions * CAP, width), (own, other))
        back = a2a(produced.reshape(positions, CAP, width)).reshape(positions * CAP, width)
        high = mix.astype(BF16)
        low = (mix - high.astype(F32)).astype(BF16)
        both = jnp.dot(jnp.concatenate([high, low]), back, preferred_element_type=F32)
        outs.append(both[: mix.shape[0]] + both[mix.shape[0] :])
    returned = lax.ppermute(outs[1][rows:].astype(BF16), "rep", swap_rep)
    second = outs[1][:rows] + returned.astype(F32)
    return jnp.stack([outs[0].astype(BF16), second.astype(BF16)])


def solution(mesh):
    return jax.shard_map(
        body,
        mesh=mesh,
        in_specs=(
            P(None, ("rep", "ep"), None),
            P(None, ("rep", "ep"), None),
            P(None, ("rep", "ep"), None),
            P(),
            P(),
            P("rep", "ep", None, None),
            P("rep", "ep", None, None),
            P("rep", "ep", None, None),
        ),
        out_specs=P(None, ("rep", "ep"), None),
        check_vma=False,
    )
```

```python
import jax
import jax.numpy as jnp
from jax import lax
from jax.experimental import pallas as pl
from jax.experimental.pallas import tpu as pltpu
from jax.sharding import PartitionSpec as P

CAP = 8
BF16 = jnp.bfloat16
F32 = jnp.float32
NY, NZ, NX = 4, 8, 2
PLANE = NY * NX
PAIRS = 4
UNIT = 2 * CAP
META = NZ * 32
MESH = pl.DeviceIdType.MESH
MIB = 1 << 20


def token_block(tokens, experts, gates, layout, allowed):
    hit = (experts[:, :, None] == layout[None, None, :]) & allowed[None, None, :]
    named = jnp.any(hit, axis=1)
    weight = jnp.sum(jnp.where(hit, gates[:, :, None], 0.0), axis=1)
    count = experts.shape[0]
    before = jnp.tril(jnp.ones((count, count), BF16), -1)
    rank = jnp.dot(before, named.astype(BF16), preferred_element_type=F32)
    rank = jnp.where(named, rank, -1.0).astype(BF16)
    high = lax.reduce_precision(weight, 8, 7)
    low = (weight - high).astype(BF16)
    kinds = jnp.stack([rank, high.astype(BF16), low, jnp.zeros_like(rank)], axis=1)
    kinds = kinds.reshape(count, 4, NY, NZ, NX).transpose(0, 3, 1, 2, 4)
    return jnp.concatenate([tokens, kinds.reshape(count, META)], axis=1)


def kernel(
    tb0, tb1, tbx, gate_hbm, up_hbm, down_hbm, out,
    wg, wu, wd, g0, g1, s0, s1, r0, r1, t0, t1, q0, q1, w0, w1, acc0, acc1, hid, sel, swap,
    load_sem, wsend, wrecv, own_sem, xsend, xrecv,
    gsend, grecv, dsend, drecv, dloc, csend, crecv, cloc, rsend, rrecv,
):
    width = out.shape[2]
    half = width // 2
    ghalf = (width + META) // 2
    tile = 512
    rep = lax.axis_index("rep")
    ep = lax.axis_index("ep")
    core = lax.rem(ep, 2)
    x = lax.rem(lax.div(ep, 2), NX)
    z = lax.rem(lax.div(ep, 2 * NX), NZ)
    y = lax.div(ep, 2 * NX * NZ)
    here = y * NX + x

    def at(yy, zz, xx):
        return (rep, ((yy * NZ + zz) * NX + xx) * 2 + core)

    right = at(y, lax.rem(z + 1, NZ), x)
    left = at(y, lax.rem(z + NZ - 1, NZ), x)
    other_rep = (1 - rep, ep)
    other_core = (rep, ep + 1 - 2 * core)
    plane = []
    for d in range(1, PLANE):
        yy, xx = lax.rem(y + d // NX, NY), lax.rem(x + d % NX, NX)
        plane.append((yy * NX + xx, at(yy, z, xx)))

    barrier = pltpu.get_barrier_semaphore()
    partners = [right, left, other_rep, other_core] + [dev for _, dev in plane]
    for dev in partners:
        pl.semaphore_signal(barrier, inc=1, device_id=dev, device_id_type=MESH)
    pl.semaphore_wait(barrier, len(partners))

    def remote(src, dst, send, recv, dev):
        return pltpu.make_async_remote_copy(
            src_ref=src, dst_ref=dst, send_sem=send, recv_sem=recv, device_id=dev, device_id_type=MESH
        )

    def unit(p, j):
        return pl.ds(pl.multiple_of(j * PLANE * UNIT + p * UNIT, UNIT), UNIT)

    rows_of = (32, 64)
    G, S, R, T, Q, W, ACC = (g0, g1), (s0, s1), (r0, r1), (t0, t1), (q0, q1), (w0, w1), (acc0, acc1)

    def ring_out(b, k):
        n = rows_of[b]
        g = G[b]
        first, second = pl.ds(0, n), pl.ds(n, n)
        if k == 1:
            src_r, src_l = g.at[3, first], g.at[3, first]
        elif k < 4:
            src_r, src_l = g.at[k - 2, first], g.at[k - 2, second]
        else:
            src_r = g.at[2, first, pl.ds(0, ghalf)]
            src_l = g.at[2, second, pl.ds(ghalf, ghalf)]
        if k < 4:
            dst_r, dst_l = g.at[k - 1, first], g.at[k - 1, second]
        else:
            dst_r = g.at[3, second, pl.ds(0, ghalf)]
            dst_l = g.at[3, second, pl.ds(ghalf, ghalf)]
        return (
            remote(src_r, dst_r, gsend.at[b, k - 1, 0], grecv.at[b, k - 1, 0], right),
            remote(src_l, dst_l, gsend.at[b, k - 1, 1], grecv.at[b, k - 1, 1], left),
        )

    def ring_start(b, k):
        for copy in ring_out(b, k):
            copy.start()

    def dispatch_copies(b, j):
        remotes = [
            remote(S[b].at[unit(p, j)], R[b].at[unit(here, j)], dsend.at[b, j, d], drecv.at[b, j, d], dev)
            for d, (p, dev) in enumerate(plane)
        ]
        return remotes, pltpu.make_async_copy(S[b].at[unit(here, j)], R[b].at[unit(here, j)], dloc.at[b, j])

    def pack(b, j):
        n = rows_of[b]
        g, s, w = G[b], S[b], W[b]
        meta = jnp.dot(g[j, :, width:], sel[...], preferred_element_type=F32)
        lane = lax.broadcasted_iota(jnp.int32, (2 * n, 128), 1)
        row = lax.broadcasted_iota(jnp.int32, (2 * n, 128), 0)
        fits = (meta[:, :128] == (lane & 7).astype(F32)) & (((lane >> 3) & 1) == (row >= n).astype(jnp.int32))
        w[j, : 2 * n] = jnp.where(fits, meta[:, 128:256], 0.0).astype(BF16)
        w[j, 2 * n :] = jnp.where(fits, meta[:, 256:], 0.0).astype(BF16)
        pick = jnp.where(fits, 1.0, 0.0).T.astype(BF16)

        @pl.loop(0, width // tile)
        def _(i):
            cols = pl.ds(pl.multiple_of(i * tile, tile), tile)
            s[pl.ds(j * PLANE * UNIT, PLANE * UNIT), cols] = jnp.dot(
                pick, g[j, :, cols], preferred_element_type=F32
            ).astype(BF16)

        remotes, local = dispatch_copies(b, j)
        for copy in remotes:
            copy.start()
        local.start()

    def dispatch_wait(b, j):
        remotes, local = dispatch_copies(b, j)
        for copy in remotes:
            copy.wait_recv()
        local.wait()

    def gather_step(b, k):
        for copy in ring_out(b, k):
            copy.wait_recv()
        if k < 4:
            ring_start(b, k + 1)

    def ffn(b, m):
        rows = pl.ds(m * 256, 256)
        r = R[b]

        @pl.loop(0, 4)
        def _(i):
            h = lax.div(i, 2)
            cols = pl.ds(pl.multiple_of(lax.rem(i, 2) * 256, 256), 256)
            gate = jnp.dot(r[rows, :], wg[h, :, cols], preferred_element_type=F32)
            up = jnp.dot(r[rows, :], wu[h, :, cols], preferred_element_type=F32)
            hid[:, pl.ds(pl.multiple_of(i * 256, 256), 256)] = (jax.nn.silu(gate) * up).astype(BF16)

        @pl.loop(0, width // tile)
        def _(i):
            cols = pl.ds(pl.multiple_of(i * tile, tile), tile)
            down = jnp.dot(hid[:, :512], wd[0, :, cols], preferred_element_type=F32)
            down = down + jnp.dot(hid[:, 512:], wd[1, :, cols], preferred_element_type=F32)
            r[rows, cols] = down.astype(BF16)

    def return_copies(b, j):
        remotes = [
            remote(R[b].at[unit(p, j)], T[b].at[unit(here, j)], csend.at[b, j, d], crecv.at[b, j, d], dev)
            for d, (p, dev) in enumerate(plane)
        ]
        return remotes, pltpu.make_async_copy(R[b].at[unit(here, j)], T[b].at[unit(here, j)], cloc.at[b, j])

    def give_back(b, j):
        remotes, local = return_copies(b, j)
        for copy in remotes:
            copy.start()
        local.start()

    def sum_out(b, k):
        q = Q[b]
        lo, hi = pl.ds(0, half), pl.ds(half, half)
        if k == 4:
            pairs = ((q.at[8, :, lo], q.at[3, :, lo]), (q.at[8, :, hi], q.at[7, :, hi]))
        else:
            pairs = ((q.at[k], q.at[k - 1]), (q.at[4 + k], q.at[3 + k]))
        return tuple(
            remote(src, dst, rsend.at[b, k - 1, i], rrecv.at[b, k - 1, i], dev)
            for i, ((src, dst), dev) in enumerate(zip(pairs, (right, left)))
        )

    def combine_step(b, k):
        n = rows_of[b]
        q, t, w = Q[b], T[b], W[b]
        j = k - 1
        remotes, local = return_copies(b, j)
        for copy in remotes:
            copy.wait_recv()
        local.wait()
        if k < 4:
            for copy in sum_out(b, k + 1):
                copy.wait_recv()
        for first in range(0, width, half):

            @pl.loop(0, half // 256)
            def _(i):
                cols = pl.ds(pl.multiple_of(first + i * 256, 256), 256)
                both = jnp.dot(
                    w[j], t[pl.ds(j * PLANE * UNIT, PLANE * UNIT), cols], preferred_element_type=F32
                )
                part = both[: 2 * n] + both[2 * n :]
                if k == 4:
                    ACC[b][:, cols] = part[:n]
                    q[8, :, cols] = part[n:].astype(BF16)
                else:
                    to_left, to_right = part[:n], part[n:]
                    if k < 3 or first == 0:
                        to_right = to_right + q[k, :, cols].astype(F32)
                    if k < 3 or first > 0:
                        to_left = to_left + q[4 + k, :, cols].astype(F32)
                    q[k, :, cols] = to_right.astype(BF16)
                    q[4 + k, :, cols] = to_left.astype(BF16)

        for copy in sum_out(b, k):
            copy.start()

    def last_sum(b):
        for copy in sum_out(b, 1):
            copy.wait_recv()

    own0 = pltpu.make_async_copy(tb0, g0.at[3, pl.ds(0, 32)], own_sem.at[0])
    own1 = pltpu.make_async_copy(tb1, g1.at[3, pl.ds(0, 32)], own_sem.at[1])
    partner_in = remote(tbx, g1.at[3, pl.ds(32, 32)], xsend.at[0], xrecv.at[0], other_rep)
    own0.start()
    partner_in.start()
    own1.start()
    own0.wait()
    ring_start(0, 1)
    loads = [
        pltpu.make_async_copy(src, dst.at[0], load_sem.at[i])
        for i, (src, dst) in enumerate(((gate_hbm, wg), (up_hbm, wu), (down_hbm, wd)))
    ]
    pushes = [
        remote(src, dst.at[1], wsend.at[i], wrecv.at[i], other_core)
        for i, (src, dst) in enumerate(((gate_hbm, wg), (up_hbm, wu), (down_hbm, wd)))
    ]
    for copy in pushes + loads:
        copy.start()

    srow = lax.broadcasted_iota(jnp.int32, (META, 384), 0)
    scol = lax.broadcasted_iota(jnp.int32, (META, 384), 1)
    chosen = ((srow >> 5) == z) & (((srow >> 3) & 3) == (scol >> 7)) & ((srow & 7) == ((scol & 127) >> 4))
    sel[...] = jnp.where(chosen, 1.0, 0.0).astype(BF16)

    for k in range(1, 5):
        gather_step(0, k)
        if k == 4:
            own1.wait()
            partner_in.wait_recv()
            ring_start(1, 1)
        pack(0, k - 1)

    gather_step(1, 1)
    pack(1, 0)
    for copy in loads:
        copy.wait()
    for copy in pushes:
        copy.wait_recv()
    dispatch_wait(0, 0)
    dispatch_wait(0, 1)
    ffn(0, 0)
    gather_step(1, 2)
    pack(1, 1)
    gather_step(1, 3)
    pack(1, 2)
    dispatch_wait(0, 2)
    dispatch_wait(0, 3)
    ffn(0, 1)
    gather_step(1, 4)
    pack(1, 3)
    for j in (3, 2, 1, 0):
        give_back(0, j)
    dispatch_wait(1, 0)
    dispatch_wait(1, 1)
    ffn(1, 0)
    combine_step(0, 4)
    dispatch_wait(1, 2)
    dispatch_wait(1, 3)
    ffn(1, 1)
    for j in (3, 2, 1, 0):
        give_back(1, j)
    combine_step(0, 3)
    combine_step(0, 2)
    combine_step(0, 1)
    combine_step(1, 4)
    last_sum(0)
    out[0] = (acc0[...] + q0[0].astype(F32) + q0[4].astype(F32)).astype(BF16)
    combine_step(1, 3)
    combine_step(1, 2)
    combine_step(1, 1)
    last_sum(1)
    swap[0] = (acc1[32:, :] + q1[0, 32:].astype(F32) + q1[4, 32:].astype(F32)).astype(BF16)
    back = remote(swap.at[0], swap.at[1], xsend.at[1], xrecv.at[1], other_rep)
    back.start()
    acc1[:32, :] = acc1[:32, :] + q1[0, :32].astype(F32) + q1[4, :32].astype(F32)
    back.wait_recv()
    out[1] = (acc1[:32, :] + swap[1].astype(F32)).astype(BF16)

    back.wait_send()
    partner_in.wait_send()
    for copy in pushes:
        copy.wait_send()
    for b in range(2):
        for k in range(1, 5):
            for copy in ring_out(b, k) + sum_out(b, k):
                copy.wait_send()
        for j in range(PAIRS):
            for copy in dispatch_copies(b, j)[0] + return_copies(b, j)[0]:
                copy.wait_send()


def body(tokens, routing, route_gate, place_old, place_new, gate_proj, up_proj, down_proj):
    rep = lax.axis_index("rep")
    batches, rows, width = tokens.shape
    ff = gate_proj.shape[3]
    old_here = lax.dynamic_index_in_dim(place_old, rep, 0, keepdims=False)
    new_here = lax.dynamic_index_in_dim(place_new, rep, 0, keepdims=False)
    old_there = lax.dynamic_index_in_dim(place_old, 1 - rep, 0, keepdims=False)
    new_there = lax.dynamic_index_in_dim(place_new, 1 - rep, 0, keepdims=False)
    always = jnp.ones_like(old_here, dtype=bool)
    tb0 = token_block(tokens[0], routing[0], route_gate[0], old_here, always)
    tb1 = token_block(tokens[1], routing[1], route_gate[1], old_here, new_here == old_here)
    tbx = token_block(tokens[1], routing[1], route_gate[1], old_there, new_there != old_there)

    slots = PAIRS * PLANE * UNIT
    wide = width + META
    vm = pltpu.VMEM
    dma = pltpu.SemaphoreType.DMA
    anywhere = pl.BlockSpec(memory_space=pl.ANY)
    return pl.pallas_call(
        kernel,
        out_shape=jax.ShapeDtypeStruct((batches, rows, width), BF16),
        in_specs=[anywhere] * 6,
        out_specs=pl.BlockSpec(memory_space=pltpu.VMEM),
        scratch_shapes=[
            vm((2, width, ff), BF16),
            vm((2, width, ff), BF16),
            vm((2, ff, width), BF16),
            vm((PAIRS, 2 * rows, wide), BF16),
            vm((PAIRS, 4 * rows, wide), BF16),
            vm((slots, width), BF16),
            vm((slots, width), BF16),
            vm((slots, width), BF16),
            vm((slots, width), BF16),
            vm((slots, width), BF16),
            vm((slots, width), BF16),
            vm((9, rows, width), BF16),
            vm((9, 2 * rows, width), BF16),
            vm((PAIRS, 4 * rows, 128), BF16),
            vm((PAIRS, 8 * rows, 128), BF16),
            vm((rows, width), F32),
            vm((2 * rows, width), F32),
            vm((256, 2 * ff), BF16),
            vm((META, 384), BF16),
            vm((2, rows, width), BF16),
            dma((3,)),
            dma((3,)),
            dma((3,)),
            dma((2,)),
            dma((2,)),
            dma((2,)),
            dma((2, 4, 2)),
            dma((2, 4, 2)),
            dma((2, PAIRS, 7)),
            dma((2, PAIRS, 7)),
            dma((2, PAIRS)),
            dma((2, PAIRS, 7)),
            dma((2, PAIRS, 7)),
            dma((2, PAIRS)),
            dma((2, 4, 2)),
            dma((2, 4, 2)),
        ],
        compiler_params=pltpu.CompilerParams(
            collective_id=0, has_side_effects=True, vmem_limit_bytes=62 * MIB
        ),
        name="expert_layer",
    )(tb0, tb1, tbx, gate_proj[0, 0], up_proj[0, 0], down_proj[0, 0])


def solution(mesh):
    return jax.shard_map(
        body,
        mesh=mesh,
        in_specs=(
            P(None, ("rep", "ep"), None),
            P(None, ("rep", "ep"), None),
            P(None, ("rep", "ep"), None),
            P(),
            P(),
            P("rep", "ep", None, None),
            P("rep", "ep", None, None),
            P("rep", "ep", None, None),
        ),
        out_specs=P(None, ("rep", "ep"), None),
        check_vma=False,
    )
```

```python
import jax
import jax.numpy as jnp
from jax import lax
from jax.experimental import pallas as pl
from jax.experimental.pallas import tpu as pltpu
from jax.sharding import PartitionSpec as P

CAP = 8
BF16 = jnp.bfloat16
F32 = jnp.float32
NY, NZ, NX = 4, 8, 2
PLANE = NY * NX
PAIRS = 4
UNIT = 2 * CAP
META = 256
MESH = pl.DeviceIdType.MESH
MIB = 1 << 20


def kernel(
    tokens, routing, route_gate, places, gate_hbm, up_hbm, down_hbm, out,
    wg, wu, wd, g0, g1, s0, s1, r0, r1, t0, t1, q0, q1, w0, w1, acc0, acc1, hid, sel, swap, theirs,
    load_sem, wsend, wrecv, own_sem, xsend, xrecv,
    gsend, grecv, dsend, drecv, dloc, csend, crecv, cloc, rsend, rrecv,
):
    width = out.shape[2]
    wide = width + META
    half = width // 2
    tile = 512
    rows_of = (32, 64)
    block = PLANE * UNIT
    rep = lax.axis_index("rep")
    ep = lax.axis_index("ep")
    core = lax.rem(ep, 2)
    x = lax.rem(lax.div(ep, 2), NX)
    z = lax.rem(lax.div(ep, 2 * NX), NZ)
    y = lax.div(ep, 2 * NX * NZ)
    here = y * NX + x
    def at(yy, zz, xx):
        return (rep, ((yy * NZ + zz) * NX + xx) * 2 + core)

    right = at(y, lax.rem(z + 1, NZ), x)
    left = at(y, lax.rem(z + NZ - 1, NZ), x)
    other_rep = (1 - rep, ep)
    other_core = (rep, ep + 1 - 2 * core)
    plane = []
    for d in range(1, PLANE):
        yy, xx = lax.rem(y + d // NX, NY), lax.rem(x + d % NX, NX)
        plane.append((yy * NX + xx, at(yy, z, xx)))

    barrier = pltpu.get_barrier_semaphore()
    partners = [right, left, other_rep, other_core] + [dev for _, dev in plane]
    for dev in partners:
        pl.semaphore_signal(barrier, inc=1, device_id=dev, device_id_type=MESH)
    mine = pl.ds(0, 32)
    own = [
        pltpu.make_async_copy(tokens.at[b], g.at[3, mine, pl.ds(0, width)], own_sem.at[b])
        for b, g in enumerate((g0, g1))
    ]
    for copy in own:
        copy.start()

    first = rep == 0
    old_here = jnp.where(first, places[0:1, :], places[1:2, :])
    old_there = jnp.where(first, places[1:2, :], places[0:1, :])
    moved_here = old_here != jnp.where(first, places[2:3, :], places[3:4, :])
    moved_there = old_there != jnp.where(first, places[3:4, :], places[2:3, :])
    before = (
        lax.broadcasted_iota(jnp.int32, (32, 32), 0) > lax.broadcasted_iota(jnp.int32, (32, 32), 1)
    ).astype(F32)
    lower = lax.broadcasted_iota(jnp.int32, (32, 128), 1) < 64

    def describe(b, layout, served, ref):
        weight = jnp.zeros((32, 128), F32)
        named = jnp.zeros((32, 128), F32)
        for k in range(routing.shape[2]):
            hit = (routing[b, :, k : k + 1] == layout) & served
            weight = weight + jnp.where(hit, route_gate[b, :, k : k + 1], 0.0)
            named = named + jnp.where(hit, 1.0, 0.0)
        rank = jnp.dot(before.astype(BF16), named.astype(BF16), preferred_element_type=F32)
        rank = jnp.where(named > 0.5, rank, -1.0)
        high = weight.astype(BF16).astype(F32)
        ref[:, :128] = jnp.where(lower, rank, high).astype(BF16)
        ref[:, 128:] = jnp.where(lower, weight - high, 0.0).astype(BF16)

    lanes = pl.ds(width, META)
    describe(0, old_here, old_here >= 0, g0.at[3, mine, lanes])
    describe(1, old_here, ~moved_here, g1.at[3, mine, lanes])
    describe(1, old_there, moved_there, theirs)
    pl.semaphore_wait(barrier, len(partners))

    def remote(src, dst, send, recv, dev):
        return pltpu.make_async_remote_copy(
            src_ref=src, dst_ref=dst, send_sem=send, recv_sem=recv, device_id=dev, device_id_type=MESH
        )

    def unit(p, j, count=UNIT):
        return pl.ds(pl.multiple_of(j * block + p * UNIT, UNIT), count)

    G, S, R, T, Q, W, ACC = (g0, g1), (s0, s1), (r0, r1), (t0, t1), (q0, q1), (w0, w1), (acc0, acc1)

    def ways(k, c):
        return (0, 1) if k < 4 else (c,)

    def ring(b, k, way, c):
        g, n = G[b], rows_of[b]
        chunk = n // 2
        src = g.at[3, pl.ds(c * chunk, chunk)] if k == 1 else g.at[k - 2, pl.ds(way * n + c * chunk, chunk)]
        dst = g.at[k - 1, pl.ds((way if k < 4 else 1) * n + c * chunk, chunk)]
        sems = (gsend.at[b, k - 1, way, c], grecv.at[b, k - 1, way, c])
        return remote(src, dst, *sems, left if way else right)

    def ring_start(b, c):
        for way in ways(1, c):
            ring(b, 1, way, c).start()

    def gather_step(b, k):
        for c in range(2):
            for way in ways(k, c):
                ring(b, k, way, c).wait_recv()
                if k < 4 and way in ways(k + 1, c):
                    ring(b, k + 1, way, c).start()

    def dispatch_copies(b, j):
        remotes = [
            remote(S[b].at[unit(p, j)], R[b].at[unit(here, j)], dsend.at[b, j, d], drecv.at[b, j, d], dev)
            for d, (p, dev) in enumerate(plane)
        ]
        return remotes, pltpu.make_async_copy(S[b].at[unit(here, j)], R[b].at[unit(here, j)], dloc.at[b, j])

    def pack(b, j):
        g, s, w, n = G[b], S[b], W[b], rows_of[b]
        meta = jnp.dot(g[j, :, width:], sel[...], preferred_element_type=F32)
        lane = lax.broadcasted_iota(jnp.int32, (2 * n, 128), 1)
        row = lax.broadcasted_iota(jnp.int32, (2 * n, 128), 0)
        fits = (meta[:, :128] == (lane & 7).astype(F32)) & (((lane >> 3) & 1) == (row >= n).astype(jnp.int32))
        w[j, : 2 * n] = jnp.where(fits, meta[:, 128:256], 0.0).astype(BF16)
        w[j, 2 * n :] = jnp.where(fits, meta[:, 256:], 0.0).astype(BF16)
        pick = jnp.where(fits, 1.0, 0.0).T.astype(BF16)

        @pl.loop(0, width // tile)
        def _(i):
            cols = pl.ds(pl.multiple_of(i * tile, tile), tile)
            s[pl.ds(j * block, block), cols] = jnp.dot(
                pick, g[j, :, cols], preferred_element_type=F32
            ).astype(BF16)

        remotes, local = dispatch_copies(b, j)
        for copy in remotes:
            copy.start()
        local.start()

    def dispatch_wait(b, j):
        remotes, local = dispatch_copies(b, j)
        for copy in remotes:
            copy.wait_recv()
        local.wait()

    def ffn(b, m):
        rows = pl.ds(m * 256, 256)
        r = R[b]

        @pl.loop(0, 4)
        def _(i):
            h = lax.div(i, 2)
            cols = pl.ds(pl.multiple_of(lax.rem(i, 2) * 256, 256), 256)
            gate = jnp.dot(r[rows, :], wg[h, :, cols], preferred_element_type=F32)
            up = jnp.dot(r[rows, :], wu[h, :, cols], preferred_element_type=F32)
            hid[:, pl.ds(pl.multiple_of(i * 256, 256), 256)] = (jax.nn.silu(gate) * up).astype(BF16)

        @pl.loop(0, width // tile)
        def _(i):
            cols = pl.ds(pl.multiple_of(i * tile, tile), tile)
            down = jnp.dot(hid[:, :512], wd[0, :, cols], preferred_element_type=F32)
            down = down + jnp.dot(hid[:, 512:], wd[1, :, cols], preferred_element_type=F32)
            r[rows, cols] = down.astype(BF16)

    def return_copies(b, j):
        remotes = [
            remote(R[b].at[unit(p, j)], T[b].at[unit(here, j)], csend.at[b, j, d], crecv.at[b, j, d], dev)
            for d, (p, dev) in enumerate(plane)
        ]
        return remotes, [pltpu.make_async_copy(R[b].at[unit(here, j)], T[b].at[unit(here, j)], cloc.at[b, j])]

    def give_back(b, j):
        remotes, locals_ = return_copies(b, j)
        for copy in remotes + locals_:
            copy.start()

    def sums(b, k, h):
        q = Q[b]
        cols = pl.ds(h * half, half)
        copies = []
        for way in ways(k, h):
            src = q.at[8, :, cols] if k == 4 else q.at[4 * way + k, :, cols]
            dst = q.at[4 * way + k - 1, :, cols]
            sems = (rsend.at[b, k - 1, way, h], rrecv.at[b, k - 1, way, h])
            copies.append(remote(src, dst, *sems, left if way else right))
        return copies

    def combine_step(b, k, then=()):
        q, t, w, n = Q[b], T[b], W[b], rows_of[b]
        j = k - 1
        remotes, locals_ = return_copies(b, j)
        for copy in remotes:
            copy.wait_recv()
        for copy in locals_:
            copy.wait()
        for later in then:
            give_back(*later)
        for h in range(2):
            if k < 4:
                for copy in sums(b, k + 1, h):
                    copy.wait_recv()

            @pl.loop(0, half // 256)
            def _(i):
                cols = pl.ds(pl.multiple_of(h * half + i * 256, 256), 256)
                both = jnp.dot(w[j], t[pl.ds(j * block, block), cols], preferred_element_type=F32)
                part = both[: 2 * n] + both[2 * n :]
                if k == 4:
                    ACC[b][:, cols] = part[:n]
                    q[8, :, cols] = part[n:].astype(BF16)
                else:
                    to_left, to_right = part[:n], part[n:]
                    if k < 3 or h == 0:
                        to_right = to_right + q[k, :, cols].astype(F32)
                    if k < 3 or h == 1:
                        to_left = to_left + q[4 + k, :, cols].astype(F32)
                    q[k, :, cols] = to_right.astype(BF16)
                    q[4 + k, :, cols] = to_left.astype(BF16)

            for copy in sums(b, k, h):
                copy.start()

    def arrived(b):
        for h in range(2):
            for copy in sums(b, 1, h):
                copy.wait_recv()

    swap_in = [
        remote(tokens.at[1], g1.at[3, pl.ds(32, 32), pl.ds(0, width)], xsend.at[0], xrecv.at[0], other_rep),
        remote(theirs, g1.at[3, pl.ds(32, 32), lanes], xsend.at[1], xrecv.at[1], other_rep),
    ]
    swap_out = remote(swap.at[0], swap.at[1], xsend.at[2], xrecv.at[2], other_rep)
    for copy in own:
        copy.wait()
    ring_start(0, 0)
    ring_start(0, 1)
    for copy in swap_in:
        copy.start()
    loads = [
        pltpu.make_async_copy(src, dst.at[0], load_sem.at[i])
        for i, (src, dst) in enumerate(((gate_hbm, wg), (up_hbm, wu), (down_hbm, wd)))
    ]
    pushes = [
        remote(src, dst.at[1], wsend.at[i], wrecv.at[i], other_core)
        for i, (src, dst) in enumerate(((gate_hbm, wg), (up_hbm, wu), (down_hbm, wd)))
    ]
    for copy in pushes + loads:
        copy.start()

    lane_of = lax.broadcasted_iota(jnp.int32, (META, 384), 0)
    slot = lax.broadcasted_iota(jnp.int32, (META, 384), 1)
    place = lane_of & 63
    chosen = ((lane_of >> 6) == (slot >> 7)) & (((place >> 1) & (NZ - 1)) == z)
    chosen = chosen & (NX * (place >> 4) + (place & 1) == ((slot & 127) >> 4))
    sel[...] = jnp.where(chosen, 1.0, 0.0).astype(BF16)

    for k in range(1, 5):
        gather_step(0, k)
        if k == 3:
            for copy in swap_in:
                copy.wait_recv()
            ring_start(1, 0)
            ring_start(1, 1)
        pack(0, k - 1)

    gather_step(1, 1)
    pack(1, 0)
    for copy in loads:
        copy.wait()
    for copy in pushes:
        copy.wait_recv()
    dispatch_wait(0, 0)
    dispatch_wait(0, 1)
    ffn(0, 0)
    gather_step(1, 2)
    pack(1, 1)
    dispatch_wait(0, 2)
    dispatch_wait(0, 3)
    ffn(0, 1)
    gather_step(1, 3)
    pack(1, 2)
    gather_step(1, 4)
    pack(1, 3)
    dispatch_wait(1, 0)
    dispatch_wait(1, 1)
    give_back(0, 3)
    ffn(1, 0)
    dispatch_wait(1, 2)
    give_back(0, 2)
    dispatch_wait(1, 3)
    ffn(1, 1)
    give_back(1, 3)
    give_back(1, 2)
    combine_step(0, 4, [(1, 1)])
    combine_step(0, 3, [(1, 0)])
    combine_step(1, 4, [(0, 1)])
    combine_step(1, 3, [(0, 0)])
    combine_step(1, 2)
    combine_step(1, 1)
    combine_step(0, 2)
    arrived(1)
    swap[0] = (acc1[32:, :] + q1[0, 32:].astype(F32) + q1[4, 32:].astype(F32)).astype(BF16)
    swap_out.start()
    acc1[:32, :] = acc1[:32, :] + q1[0, :32].astype(F32) + q1[4, :32].astype(F32)
    combine_step(0, 1)
    swap_out.wait_recv()
    out[1] = (acc1[:32, :] + swap[1].astype(F32)).astype(BF16)
    arrived(0)
    out[0] = (acc0[...] + q0[0].astype(F32) + q0[4].astype(F32)).astype(BF16)

    for copy in pushes + swap_in + [swap_out]:
        copy.wait_send()
    for b in range(2):
        for k in range(1, 5):
            for c in range(2):
                for copy in [ring(b, k, way, c) for way in ways(k, c)] + sums(b, k, c):
                    copy.wait_send()
    for b in range(2):
        for j in range(PAIRS):
            for copy in dispatch_copies(b, j)[0] + return_copies(b, j)[0]:
                copy.wait_send()


def body(tokens, routing, route_gate, place_old, place_new, gate_proj, up_proj, down_proj):
    batches, rows, width = tokens.shape
    ff = gate_proj.shape[3]
    places = jnp.concatenate([place_old, place_new])
    places = jnp.concatenate([places, places], axis=1)

    slots = PAIRS * PLANE * UNIT
    wide = width + META
    vm = pltpu.VMEM
    dma = pltpu.SemaphoreType.DMA
    anywhere = pl.BlockSpec(memory_space=pl.ANY)
    local = pl.BlockSpec(memory_space=pltpu.VMEM)
    return pl.pallas_call(
        kernel,
        out_shape=jax.ShapeDtypeStruct((batches, rows, width), BF16),
        in_specs=[anywhere, local, local, local, anywhere, anywhere, anywhere],
        out_specs=local,
        scratch_shapes=[
            vm((2, width, ff), BF16),
            vm((2, width, ff), BF16),
            vm((2, ff, width), BF16),
            vm((PAIRS, 2 * rows, wide), BF16),
            vm((PAIRS, 4 * rows, wide), BF16),
            vm((slots, width), BF16),
            vm((slots, width), BF16),
            vm((slots, width), BF16),
            vm((slots, width), BF16),
            vm((slots, width), BF16),
            vm((slots, width), BF16),
            vm((9, rows, width), BF16),
            vm((9, 2 * rows, width), BF16),
            vm((PAIRS, 4 * rows, 128), BF16),
            vm((PAIRS, 8 * rows, 128), BF16),
            vm((rows, width), F32),
            vm((2 * rows, width), F32),
            vm((256, 2 * ff), BF16),
            vm((META, 384), BF16),
            vm((2, rows, width), BF16),
            vm((rows, META), BF16),
            dma((3,)),
            dma((3,)),
            dma((3,)),
            dma((2,)),
            dma((3,)),
            dma((3,)),
            dma((2, 4, 2, 2)),
            dma((2, 4, 2, 2)),
            dma((2, PAIRS, 7)),
            dma((2, PAIRS, 7)),
            dma((2, PAIRS)),
            dma((2, PAIRS, 7)),
            dma((2, PAIRS, 7)),
            dma((2, PAIRS)),
            dma((2, 4, 2, 2)),
            dma((2, 4, 2, 2)),
        ],
        compiler_params=pltpu.CompilerParams(
            collective_id=0, has_side_effects=True, vmem_limit_bytes=62 * MIB
        ),
        name="expert_layer",
    )(tokens, routing, route_gate, places, gate_proj[0, 0], up_proj[0, 0], down_proj[0, 0])


def solution(mesh):
    return jax.shard_map(
        body,
        mesh=mesh,
        in_specs=(
            P(None, ("rep", "ep"), None),
            P(None, ("rep", "ep"), None),
            P(None, ("rep", "ep"), None),
            P(),
            P(),
            P("rep", "ep", None, None),
            P("rep", "ep", None, None),
            P("rep", "ep", None, None),
        ),
        out_specs=P(None, ("rep", "ep"), None),
        check_vma=False,
    )
```

```python
import jax
import jax.numpy as jnp
from jax import lax
from jax.experimental import pallas as pl
from jax.experimental.pallas import tpu as pltpu
from jax.sharding import PartitionSpec as P

CAP = 8
BF16 = jnp.bfloat16
F32 = jnp.float32
NY, NZ, NX = 4, 8, 2
PLANE = NY * NX
PAIRS = 4
UNIT = 2 * CAP
META = 256
MESH = pl.DeviceIdType.MESH
MIB = 1 << 20


def kernel(
    tokens, routing, route_gate, place_old, place_new, gate_hbm, up_hbm, down_hbm, out,
    wg, wu, wd, g0, g1, s0, s1, r0, r1, t0, t1, q0, q1, w0, w1, acc0, acc1, hid, sel, swap, theirs,
    load_sem, wsend, wrecv, own_sem, xsend, xrecv,
    gsend, grecv, dsend, drecv, dloc, csend, crecv, cloc, rsend, rrecv,
):
    width = out.shape[2]
    wide = width + META
    half = width // 2
    tile = 512
    rows_of = (32, 64)
    block = PLANE * UNIT
    rep = lax.axis_index("rep")
    ep = lax.axis_index("ep")
    core = lax.rem(ep, 2)
    x = lax.rem(lax.div(ep, 2), NX)
    z = lax.rem(lax.div(ep, 2 * NX), NZ)
    y = lax.div(ep, 2 * NX * NZ)
    here = y * NX + x
    def at(yy, zz, xx):
        return (rep, ((yy * NZ + zz) * NX + xx) * 2 + core)

    right = at(y, lax.rem(z + 1, NZ), x)
    left = at(y, lax.rem(z + NZ - 1, NZ), x)
    other_rep = (1 - rep, ep)
    other_core = (rep, ep + 1 - 2 * core)
    plane = []
    for d in range(1, PLANE):
        yy, xx = lax.rem(y + d // NX, NY), lax.rem(x + d % NX, NX)
        plane.append((yy * NX + xx, at(yy, z, xx)))

    barrier = pltpu.get_barrier_semaphore()
    partners = [right, left, other_rep, other_core] + [dev for _, dev in plane]
    for dev in partners:
        pl.semaphore_signal(barrier, inc=1, device_id=dev, device_id_type=MESH)
    mine = pl.ds(0, 32)
    own = [
        pltpu.make_async_copy(tokens.at[b], g.at[3, mine, pl.ds(0, width)], own_sem.at[b])
        for b, g in enumerate((g0, g1))
    ]
    for copy in own:
        copy.start()

    first = rep == 0
    old = jnp.concatenate([place_old[...], place_old[...]], axis=1)
    new = jnp.concatenate([place_new[...], place_new[...]], axis=1)
    old_here = jnp.where(first, old[0:1], old[1:2])
    old_there = jnp.where(first, old[1:2], old[0:1])
    moved_here = old_here != jnp.where(first, new[0:1], new[1:2])
    moved_there = old_there != jnp.where(first, new[1:2], new[0:1])
    before = (
        lax.broadcasted_iota(jnp.int32, (32, 32), 0) > lax.broadcasted_iota(jnp.int32, (32, 32), 1)
    ).astype(F32)
    lower = lax.broadcasted_iota(jnp.int32, (32, 128), 1) < 64

    def describe(b, layout, served, ref):
        chosen, gates = routing[b].T, route_gate[b].T
        weight = jnp.zeros((32, 128), F32)
        named = jnp.zeros((32, 128), F32)
        for k in range(routing.shape[1]):
            hit = (chosen[:, k : k + 1] == layout) & served
            weight = weight + jnp.where(hit, gates[:, k : k + 1], 0.0)
            named = named + jnp.where(hit, 1.0, 0.0)
        rank = jnp.dot(before.astype(BF16), named.astype(BF16), preferred_element_type=F32)
        rank = jnp.where(named > 0.5, rank, -1.0)
        high = weight.astype(BF16).astype(F32)
        ref[:, :128] = jnp.where(lower, rank, high).astype(BF16)
        ref[:, 128:] = jnp.where(lower, weight - high, 0.0).astype(BF16)

    lanes = pl.ds(width, META)
    describe(0, old_here, old_here >= 0, g0.at[3, mine, lanes])
    describe(1, old_here, ~moved_here, g1.at[3, mine, lanes])
    describe(1, old_there, moved_there, theirs)
    pl.semaphore_wait(barrier, len(partners))

    def remote(src, dst, send, recv, dev):
        return pltpu.make_async_remote_copy(
            src_ref=src, dst_ref=dst, send_sem=send, recv_sem=recv, device_id=dev, device_id_type=MESH
        )

    def unit(p, j, count=UNIT):
        return pl.ds(pl.multiple_of(j * block + p * UNIT, UNIT), count)

    G, S, R, T, Q, W, ACC = (g0, g1), (s0, s1), (r0, r1), (t0, t1), (q0, q1), (w0, w1), (acc0, acc1)

    def ways(k, c):
        return (0, 1) if k < 4 else (c,)

    def ring(b, k, way, c):
        g, n = G[b], rows_of[b]
        chunk = n // 2
        src = g.at[3, pl.ds(c * chunk, chunk)] if k == 1 else g.at[k - 2, pl.ds(way * n + c * chunk, chunk)]
        dst = g.at[k - 1, pl.ds((way if k < 4 else 1) * n + c * chunk, chunk)]
        sems = (gsend.at[b, k - 1, way, c], grecv.at[b, k - 1, way, c])
        return remote(src, dst, *sems, left if way else right)

    def ring_start(b, c):
        for way in ways(1, c):
            ring(b, 1, way, c).start()

    def gather_step(b, k):
        for c in range(2):
            for way in ways(k, c):
                ring(b, k, way, c).wait_recv()
                if k < 4 and way in ways(k + 1, c):
                    ring(b, k + 1, way, c).start()

    def dispatch_copies(b, j):
        remotes = [
            remote(S[b].at[unit(p, j)], R[b].at[unit(here, j)], dsend.at[b, j, d], drecv.at[b, j, d], dev)
            for d, (p, dev) in enumerate(plane)
        ]
        return remotes, pltpu.make_async_copy(S[b].at[unit(here, j)], R[b].at[unit(here, j)], dloc.at[b, j])

    def pack(b, j):
        g, s, w, n = G[b], S[b], W[b], rows_of[b]
        meta = jnp.dot(g[j, :, width:], sel[...], preferred_element_type=F32)
        lane = lax.broadcasted_iota(jnp.int32, (2 * n, 128), 1)
        row = lax.broadcasted_iota(jnp.int32, (2 * n, 128), 0)
        fits = (meta[:, :128] == (lane & 7).astype(F32)) & (((lane >> 3) & 1) == (row >= n).astype(jnp.int32))
        w[j, : 2 * n] = jnp.where(fits, meta[:, 128:256], 0.0).astype(BF16)
        w[j, 2 * n :] = jnp.where(fits, meta[:, 256:], 0.0).astype(BF16)
        pick = jnp.where(fits, 1.0, 0.0).T.astype(BF16)

        @pl.loop(0, width // tile)
        def _(i):
            cols = pl.ds(pl.multiple_of(i * tile, tile), tile)
            s[pl.ds(j * block, block), cols] = jnp.dot(
                pick, g[j, :, cols], preferred_element_type=F32
            ).astype(BF16)

        remotes, local = dispatch_copies(b, j)
        for copy in remotes:
            copy.start()
        local.start()

    def dispatch_wait(b, j):
        remotes, local = dispatch_copies(b, j)
        for copy in remotes:
            copy.wait_recv()
        local.wait()

    def ffn(b, m):
        rows = pl.ds(m * 256, 256)
        r = R[b]

        @pl.loop(0, 4)
        def _(i):
            h = lax.div(i, 2)
            cols = pl.ds(pl.multiple_of(lax.rem(i, 2) * 256, 256), 256)
            gate = jnp.dot(r[rows, :], wg[h, :, cols], preferred_element_type=F32)
            up = jnp.dot(r[rows, :], wu[h, :, cols], preferred_element_type=F32)
            hid[:, pl.ds(pl.multiple_of(i * 256, 256), 256)] = (jax.nn.silu(gate) * up).astype(BF16)

        @pl.loop(0, width // tile)
        def _(i):
            cols = pl.ds(pl.multiple_of(i * tile, tile), tile)
            down = jnp.dot(hid[:, :512], wd[0, :, cols], preferred_element_type=F32)
            down = down + jnp.dot(hid[:, 512:], wd[1, :, cols], preferred_element_type=F32)
            r[rows, cols] = down.astype(BF16)

    def return_copies(b, j):
        remotes = [
            remote(R[b].at[unit(p, j)], T[b].at[unit(here, j)], csend.at[b, j, d], crecv.at[b, j, d], dev)
            for d, (p, dev) in enumerate(plane)
        ]
        return remotes, [pltpu.make_async_copy(R[b].at[unit(here, j)], T[b].at[unit(here, j)], cloc.at[b, j])]

    def give_back(b, j):
        remotes, locals_ = return_copies(b, j)
        for copy in remotes + locals_:
            copy.start()

    def sums(b, k, h):
        q = Q[b]
        cols = pl.ds(h * half, half)
        copies = []
        for way in ways(k, h):
            src = q.at[8, :, cols] if k == 4 else q.at[4 * way + k, :, cols]
            dst = q.at[4 * way + k - 1, :, cols]
            sems = (rsend.at[b, k - 1, way, h], rrecv.at[b, k - 1, way, h])
            copies.append(remote(src, dst, *sems, left if way else right))
        return copies

    def combine_step(b, k, then=()):
        q, t, w, n = Q[b], T[b], W[b], rows_of[b]
        j = k - 1
        remotes, locals_ = return_copies(b, j)
        for copy in remotes:
            copy.wait_recv()
        for copy in locals_:
            copy.wait()
        for later in then:
            give_back(*later)
        for h in range(2):
            if k < 4:
                for copy in sums(b, k + 1, h):
                    copy.wait_recv()

            @pl.loop(0, half // 256)
            def _(i):
                cols = pl.ds(pl.multiple_of(h * half + i * 256, 256), 256)
                both = jnp.dot(w[j], t[pl.ds(j * block, block), cols], preferred_element_type=F32)
                part = both[: 2 * n] + both[2 * n :]
                if k == 4:
                    ACC[b][:, cols] = part[:n]
                    q[8, :, cols] = part[n:].astype(BF16)
                else:
                    to_left, to_right = part[:n], part[n:]
                    if k < 3 or h == 0:
                        to_right = to_right + q[k, :, cols].astype(F32)
                    if k < 3 or h == 1:
                        to_left = to_left + q[4 + k, :, cols].astype(F32)
                    q[k, :, cols] = to_right.astype(BF16)
                    q[4 + k, :, cols] = to_left.astype(BF16)

            for copy in sums(b, k, h):
                copy.start()

    def arrived(b):
        for h in range(2):
            for copy in sums(b, 1, h):
                copy.wait_recv()

    swap_in = [
        remote(tokens.at[1], g1.at[3, pl.ds(32, 32), pl.ds(0, width)], xsend.at[0], xrecv.at[0], other_rep),
        remote(theirs, g1.at[3, pl.ds(32, 32), lanes], xsend.at[1], xrecv.at[1], other_rep),
    ]
    swap_out = remote(swap.at[0], swap.at[1], xsend.at[2], xrecv.at[2], other_rep)
    for copy in own:
        copy.wait()
    ring_start(0, 0)
    ring_start(0, 1)
    for copy in swap_in:
        copy.start()
    loads = [
        pltpu.make_async_copy(src, dst.at[0], load_sem.at[i])
        for i, (src, dst) in enumerate(((gate_hbm, wg), (up_hbm, wu), (down_hbm, wd)))
    ]
    pushes = [
        remote(src, dst.at[1], wsend.at[i], wrecv.at[i], other_core)
        for i, (src, dst) in enumerate(((gate_hbm, wg), (up_hbm, wu), (down_hbm, wd)))
    ]
    for copy in pushes + loads:
        copy.start()

    lane_of = lax.broadcasted_iota(jnp.int32, (META, 384), 0)
    slot = lax.broadcasted_iota(jnp.int32, (META, 384), 1)
    place = lane_of & 63
    chosen = ((lane_of >> 6) == (slot >> 7)) & (((place >> 1) & (NZ - 1)) == z)
    chosen = chosen & (NX * (place >> 4) + (place & 1) == ((slot & 127) >> 4))
    sel[...] = jnp.where(chosen, 1.0, 0.0).astype(BF16)

    for k in range(1, 5):
        gather_step(0, k)
        if k == 2:
            for copy in swap_in:
                copy.wait_recv()
            ring_start(1, 0)
            ring_start(1, 1)
        pack(0, k - 1)

    gather_step(1, 1)
    pack(1, 0)
    for copy in loads:
        copy.wait()
    for copy in pushes:
        copy.wait_recv()
    dispatch_wait(0, 0)
    dispatch_wait(0, 1)
    ffn(0, 0)
    gather_step(1, 2)
    pack(1, 1)
    gather_step(1, 3)
    pack(1, 2)
    gather_step(1, 4)
    pack(1, 3)
    dispatch_wait(0, 2)
    dispatch_wait(0, 3)
    ffn(0, 1)
    dispatch_wait(1, 0)
    dispatch_wait(1, 1)
    give_back(0, 3)
    ffn(1, 0)
    dispatch_wait(1, 2)
    give_back(0, 2)
    dispatch_wait(1, 3)
    ffn(1, 1)
    give_back(1, 3)
    give_back(1, 2)
    combine_step(0, 4, [(1, 1)])
    combine_step(0, 3, [(1, 0)])
    combine_step(1, 4, [(0, 1)])
    combine_step(1, 3, [(0, 0)])
    combine_step(1, 2)
    combine_step(1, 1)
    combine_step(0, 2)
    arrived(1)
    swap[0] = (acc1[32:, :] + q1[0, 32:].astype(F32) + q1[4, 32:].astype(F32)).astype(BF16)
    swap_out.start()
    acc1[:32, :] = acc1[:32, :] + q1[0, :32].astype(F32) + q1[4, :32].astype(F32)
    combine_step(0, 1)
    swap_out.wait_recv()
    out[1] = (acc1[:32, :] + swap[1].astype(F32)).astype(BF16)
    arrived(0)
    out[0] = (acc0[...] + q0[0].astype(F32) + q0[4].astype(F32)).astype(BF16)

    for copy in pushes + swap_in + [swap_out]:
        copy.wait_send()
    for b in range(2):
        for k in range(1, 5):
            for c in range(2):
                for copy in [ring(b, k, way, c) for way in ways(k, c)] + sums(b, k, c):
                    copy.wait_send()
    for b in range(2):
        for j in range(PAIRS):
            for copy in dispatch_copies(b, j)[0] + return_copies(b, j)[0]:
                copy.wait_send()


def body(tokens, routing, route_gate, place_old, place_new, gate_proj, up_proj, down_proj):
    batches, rows, width = tokens.shape
    ff = gate_proj.shape[3]

    slots = PAIRS * PLANE * UNIT
    wide = width + META
    vm = pltpu.VMEM
    dma = pltpu.SemaphoreType.DMA
    anywhere = pl.BlockSpec(memory_space=pl.ANY)
    local = pl.BlockSpec(memory_space=pltpu.VMEM)
    return pl.pallas_call(
        kernel,
        out_shape=jax.ShapeDtypeStruct((batches, rows, width), BF16),
        in_specs=[anywhere] + [local] * 4 + [anywhere] * 3,
        out_specs=local,
        scratch_shapes=[
            vm((2, width, ff), BF16),
            vm((2, width, ff), BF16),
            vm((2, ff, width), BF16),
            vm((PAIRS, 2 * rows, wide), BF16),
            vm((PAIRS, 4 * rows, wide), BF16),
            vm((slots, width), BF16),
            vm((slots, width), BF16),
            vm((slots, width), BF16),
            vm((slots, width), BF16),
            vm((slots, width), BF16),
            vm((slots, width), BF16),
            vm((9, rows, width), BF16),
            vm((9, 2 * rows, width), BF16),
            vm((PAIRS, 4 * rows, 128), BF16),
            vm((PAIRS, 8 * rows, 128), BF16),
            vm((rows, width), F32),
            vm((2 * rows, width), F32),
            vm((256, 2 * ff), BF16),
            vm((META, 384), BF16),
            vm((2, rows, width), BF16),
            vm((rows, META), BF16),
            dma((3,)),
            dma((3,)),
            dma((3,)),
            dma((2,)),
            dma((3,)),
            dma((3,)),
            dma((2, 4, 2, 2)),
            dma((2, 4, 2, 2)),
            dma((2, PAIRS, 7)),
            dma((2, PAIRS, 7)),
            dma((2, PAIRS)),
            dma((2, PAIRS, 7)),
            dma((2, PAIRS, 7)),
            dma((2, PAIRS)),
            dma((2, 4, 2, 2)),
            dma((2, 4, 2, 2)),
        ],
        compiler_params=pltpu.CompilerParams(
            collective_id=0, has_side_effects=True, vmem_limit_bytes=62 * MIB
        ),
        name="expert_layer",
    )(
        tokens,
        jnp.swapaxes(routing, 1, 2),
        jnp.swapaxes(route_gate, 1, 2),
        place_old,
        place_new,
        gate_proj[0, 0],
        up_proj[0, 0],
        down_proj[0, 0],
    )


def solution(mesh):
    return jax.shard_map(
        body,
        mesh=mesh,
        in_specs=(
            P(None, ("rep", "ep"), None),
            P(None, ("rep", "ep"), None),
            P(None, ("rep", "ep"), None),
            P(),
            P(),
            P("rep", "ep", None, None),
            P("rep", "ep", None, None),
            P("rep", "ep", None, None),
        ),
        out_specs=P(None, ("rep", "ep"), None),
        check_vma=False,
    )
```

```python
import jax
import jax.numpy as jnp
from jax import lax
from jax.experimental import pallas as pl
from jax.experimental.pallas import tpu as pltpu
from jax.sharding import PartitionSpec as P

CAP = 8
BF16 = jnp.bfloat16
F32 = jnp.float32
NY, NZ, NX = 4, 8, 2
PLANE = NY * NX
PAIRS = 4
UNIT = 2 * CAP
META = 256
MESH = pl.DeviceIdType.MESH
MIB = 1 << 20


def kernel(
    tokens, routing, route_gate, place_old, place_new, gate_hbm, up_hbm, down_hbm, out,
    wg, wu, wd, g0, g1, s0, s1, r0, r1, t0, t1, q0, q1, w0, w1, acc0, acc1, hid, sel, swap, theirs,
    load_sem, wsend, wrecv, own_sem, xsend, xrecv,
    gsend, grecv, dsend, drecv, dloc, csend, crecv, cloc, rsend, rrecv,
):
    width = out.shape[2]
    wide = width + META
    half = width // 2
    tile = 512
    rows_of = (32, 64)
    block = PLANE * UNIT
    rep = lax.axis_index("rep")
    ep = lax.axis_index("ep")
    core = lax.rem(ep, 2)
    x = lax.rem(lax.div(ep, 2), NX)
    z = lax.rem(lax.div(ep, 2 * NX), NZ)
    y = lax.div(ep, 2 * NX * NZ)
    here = y * NX + x
    def at(yy, zz, xx):
        return (rep, ((yy * NZ + zz) * NX + xx) * 2 + core)

    right = at(y, lax.rem(z + 1, NZ), x)
    left = at(y, lax.rem(z + NZ - 1, NZ), x)
    other_rep = (1 - rep, ep)
    other_core = (rep, ep + 1 - 2 * core)
    plane = []
    for d in range(1, PLANE):
        yy, xx = lax.rem(y + d // NX, NY), lax.rem(x + d % NX, NX)
        plane.append((yy * NX + xx, at(yy, z, xx)))

    barrier = pltpu.get_barrier_semaphore()
    partners = [right, left, other_rep, other_core] + [dev for _, dev in plane]
    for dev in partners:
        pl.semaphore_signal(barrier, inc=1, device_id=dev, device_id_type=MESH)
    mine = pl.ds(0, 32)
    own = [
        pltpu.make_async_copy(tokens.at[b], g.at[3, mine, pl.ds(META, width)], own_sem.at[b])
        for b, g in enumerate((g0, g1))
    ]
    for copy in own:
        copy.start()

    first = rep == 0
    old = jnp.concatenate([place_old[...], place_old[...]], axis=1)
    new = jnp.concatenate([place_new[...], place_new[...]], axis=1)
    old_here = jnp.where(first, old[0:1], old[1:2])
    old_there = jnp.where(first, old[1:2], old[0:1])
    moved_here = old_here != jnp.where(first, new[0:1], new[1:2])
    moved_there = old_there != jnp.where(first, new[1:2], new[0:1])
    before = (
        lax.broadcasted_iota(jnp.int32, (32, 32), 0) > lax.broadcasted_iota(jnp.int32, (32, 32), 1)
    ).astype(F32)
    lower = lax.broadcasted_iota(jnp.int32, (32, 128), 1) < 64

    def describe(b, layout, served, ref):
        chosen, gates = routing[b].T, route_gate[b].T
        weight = jnp.zeros((32, 128), F32)
        named = jnp.zeros((32, 128), F32)
        for k in range(routing.shape[1]):
            hit = (chosen[:, k : k + 1] == layout) & served
            weight = weight + jnp.where(hit, gates[:, k : k + 1], 0.0)
            named = named + jnp.where(hit, 1.0, 0.0)
        rank = jnp.dot(before.astype(BF16), named.astype(BF16), preferred_element_type=F32)
        rank = jnp.where(named > 0.5, rank, -1.0)
        high = weight.astype(BF16).astype(F32)
        ref[:, :128] = jnp.where(lower, rank, high).astype(BF16)
        ref[:, 128:] = jnp.where(lower, weight - high, 0.0).astype(BF16)

    lanes = pl.ds(0, META)
    describe(0, old_here, old_here >= 0, g0.at[3, mine, lanes])
    describe(1, old_here, ~moved_here, g1.at[3, mine, lanes])
    describe(1, old_there, moved_there, theirs)
    pl.semaphore_wait(barrier, len(partners))

    def remote(src, dst, send, recv, dev):
        return pltpu.make_async_remote_copy(
            src_ref=src, dst_ref=dst, send_sem=send, recv_sem=recv, device_id=dev, device_id_type=MESH
        )

    def unit(p, j, count=UNIT):
        return pl.ds(pl.multiple_of(j * block + p * UNIT, UNIT), count)

    G, S, R, T, Q, W, ACC = (g0, g1), (s0, s1), (r0, r1), (t0, t1), (q0, q1), (w0, w1), (acc0, acc1)

    def ways(k, c):
        return (0, 1) if k < 4 else (c,)

    def ring(b, k, way, c):
        g, n = G[b], rows_of[b]
        cols = pl.ds(META + half, half) if c else pl.ds(0, META + half)
        src = g.at[3, pl.ds(0, n), cols] if k == 1 else g.at[k - 2, pl.ds(way * n, n), cols]
        dst = g.at[k - 1, pl.ds((way if k < 4 else 1) * n, n), cols]
        sems = (gsend.at[b, k - 1, way, c], grecv.at[b, k - 1, way, c])
        return remote(src, dst, *sems, left if way else right)

    def ring_start(b, c):
        for way in ways(1, c):
            ring(b, 1, way, c).start()

    def gather_chunk(b, k, c):
        for way in ways(k, c):
            ring(b, k, way, c).wait_recv()
            if k < 4 and way in ways(k + 1, c):
                ring(b, k + 1, way, c).start()

    def gather_step(b, k):
        gather_chunk(b, k, 0)
        gather_chunk(b, k, 1)

    def parts(b, j):
        return 2 if (b, j) == (0, 0) else 1

    def exchange(src, dst, sems, b, j, part):
        send, recv, loc = sems
        cols = pl.ds(part * half, half) if parts(b, j) == 2 else pl.ds(0, width)
        to = dst.at[unit(here, j), cols]
        remotes = [
            remote(src.at[unit(p, j), cols], to, send.at[b, j, 7 * part + d], recv.at[b, j, 7 * part + d], dev)
            for d, (p, dev) in enumerate(plane)
        ]
        return remotes, pltpu.make_async_copy(src.at[unit(here, j), cols], to, loc.at[b, j, part])

    def dispatch_copies(b, j, part):
        return exchange(S[b], R[b], (dsend, drecv, dloc), b, j, part)

    def begin(copies):
        remotes, local = copies
        for copy in remotes:
            copy.start()
        local.start()

    def landed(copies):
        remotes, local = copies
        for copy in remotes:
            copy.wait_recv()
        local.wait()

    def choose(b, j):
        g, w, n = G[b], W[b], rows_of[b]
        meta = jnp.dot(g[j, :, :META], sel[...], preferred_element_type=F32)
        lane = lax.broadcasted_iota(jnp.int32, (2 * n, 128), 1)
        row = lax.broadcasted_iota(jnp.int32, (2 * n, 128), 0)
        fits = (meta[:, :128] == (lane & 7).astype(F32)) & (((lane >> 3) & 1) == (row >= n).astype(jnp.int32))
        w[j, : 2 * n] = jnp.where(fits, meta[:, 128:256], 0.0).astype(BF16)
        w[j, 2 * n :] = jnp.where(fits, meta[:, 256:], 0.0).astype(BF16)
        return jnp.where(fits, 1.0, 0.0).T.astype(BF16)

    def pack(b, j, part, pick):
        g, s = G[b], S[b]
        step = tile // parts(b, j)

        @pl.loop(0, width // tile)
        def _(i):
            at_col = part * half + i * step
            s[pl.ds(j * block, block), pl.ds(pl.multiple_of(at_col, 256), step)] = jnp.dot(
                pick, g[j, :, pl.ds(pl.multiple_of(META + at_col, 256), step)], preferred_element_type=F32
            ).astype(BF16)

        begin(dispatch_copies(b, j, part))

    def dispatch_wait(b, j):
        for part in range(parts(b, j)):
            landed(dispatch_copies(b, j, part))

    def ffn(b, m):
        rows = pl.ds(m * 256, 256)
        r = R[b]

        @pl.loop(0, 4)
        def _(i):
            h = lax.div(i, 2)
            cols = pl.ds(pl.multiple_of(lax.rem(i, 2) * 256, 256), 256)
            gate = jnp.dot(r[rows, :], wg[h, :, cols], preferred_element_type=F32)
            up = jnp.dot(r[rows, :], wu[h, :, cols], preferred_element_type=F32)
            hid[:, pl.ds(pl.multiple_of(i * 256, 256), 256)] = (jax.nn.silu(gate) * up).astype(BF16)

        @pl.loop(0, width // tile)
        def _(i):
            cols = pl.ds(pl.multiple_of(i * tile, tile), tile)
            down = jnp.dot(hid[:, :512], wd[0, :, cols], preferred_element_type=F32)
            down = down + jnp.dot(hid[:, 512:], wd[1, :, cols], preferred_element_type=F32)
            r[rows, cols] = down.astype(BF16)

    def return_copies(b, j, part):
        return exchange(R[b], T[b], (csend, crecv, cloc), b, j, part)

    def give_back(b, j):
        for part in range(parts(b, j)):
            begin(return_copies(b, j, part))

    def sums(b, k, h):
        q = Q[b]
        cols = pl.ds(h * half, half)
        copies = []
        for way in ways(k, h):
            src = q.at[8, :, cols] if k == 4 else q.at[4 * way + k, :, cols]
            dst = q.at[4 * way + k - 1, :, cols]
            sems = (rsend.at[b, k - 1, way, h], rrecv.at[b, k - 1, way, h])
            copies.append(remote(src, dst, *sems, left if way else right))
        return copies

    def combine_step(b, k, then=()):
        q, t, w, n = Q[b], T[b], W[b], rows_of[b]
        j = k - 1
        landed(return_copies(b, j, 0))
        for later in then:
            give_back(*later)
        for h in range(2):
            if h and parts(b, j) == 2:
                landed(return_copies(b, j, 1))
            if k < 4:
                for copy in sums(b, k + 1, h):
                    copy.wait_recv()

            @pl.loop(0, half // 256)
            def _(i):
                cols = pl.ds(pl.multiple_of(h * half + i * 256, 256), 256)
                both = jnp.dot(w[j], t[pl.ds(j * block, block), cols], preferred_element_type=F32)
                part = both[: 2 * n] + both[2 * n :]
                if k == 4:
                    ACC[b][:, cols] = part[:n]
                    q[8, :, cols] = part[n:].astype(BF16)
                else:
                    to_left, to_right = part[:n], part[n:]
                    if k < 3 or h == 0:
                        to_right = to_right + q[k, :, cols].astype(F32)
                    if k < 3 or h == 1:
                        to_left = to_left + q[4 + k, :, cols].astype(F32)
                    q[k, :, cols] = to_right.astype(BF16)
                    q[4 + k, :, cols] = to_left.astype(BF16)

            for copy in sums(b, k, h):
                copy.start()

    swap_in = [
        remote(tokens.at[1], g1.at[3, pl.ds(32, 32), pl.ds(META, width)], xsend.at[0], xrecv.at[0], other_rep),
        remote(theirs, g1.at[3, pl.ds(32, 32), lanes], xsend.at[1], xrecv.at[1], other_rep),
    ]
    swap_out = remote(swap.at[0], swap.at[1], xsend.at[2], xrecv.at[2], other_rep)
    for copy in own:
        copy.wait()
    ring_start(0, 0)
    ring_start(0, 1)
    for copy in swap_in:
        copy.start()
    loads = [
        pltpu.make_async_copy(src, dst.at[0], load_sem.at[i])
        for i, (src, dst) in enumerate(((gate_hbm, wg), (up_hbm, wu), (down_hbm, wd)))
    ]
    pushes = [
        remote(src, dst.at[1], wsend.at[i], wrecv.at[i], other_core)
        for i, (src, dst) in enumerate(((gate_hbm, wg), (up_hbm, wu), (down_hbm, wd)))
    ]
    for copy in pushes + loads:
        copy.start()

    lane_of = lax.broadcasted_iota(jnp.int32, (META, 384), 0)
    slot = lax.broadcasted_iota(jnp.int32, (META, 384), 1)
    place = lane_of & 63
    chosen = ((lane_of >> 6) == (slot >> 7)) & (((place >> 1) & (NZ - 1)) == z)
    chosen = chosen & (NX * (place >> 4) + (place & 1) == ((slot & 127) >> 4))
    sel[...] = jnp.where(chosen, 1.0, 0.0).astype(BF16)

    gather_chunk(0, 1, 0)
    pick = choose(0, 0)
    pack(0, 0, 0, pick)
    gather_chunk(0, 1, 1)
    pack(0, 0, 1, pick)
    for k in range(2, 5):
        gather_step(0, k)
        if k == 2:
            for copy in swap_in:
                copy.wait_recv()
            ring_start(1, 0)
            ring_start(1, 1)
        pack(0, k - 1, 0, choose(0, k - 1))

    gather_step(1, 1)
    pack(1, 0, 0, choose(1, 0))
    for copy in loads:
        copy.wait()
    for copy in pushes:
        copy.wait_recv()
    dispatch_wait(0, 0)
    dispatch_wait(0, 1)
    ffn(0, 0)
    gather_step(1, 2)
    pack(1, 1, 0, choose(1, 1))
    gather_step(1, 3)
    pack(1, 2, 0, choose(1, 2))
    gather_step(1, 4)
    pack(1, 3, 0, choose(1, 3))
    dispatch_wait(0, 2)
    dispatch_wait(0, 3)
    ffn(0, 1)
    dispatch_wait(1, 0)
    dispatch_wait(1, 1)
    give_back(0, 3)
    ffn(1, 0)
    dispatch_wait(1, 2)
    give_back(0, 2)
    dispatch_wait(1, 3)
    ffn(1, 1)
    give_back(1, 3)
    give_back(1, 2)
    combine_step(0, 4, [(1, 1)])
    combine_step(0, 3, [(1, 0)])
    combine_step(1, 4, [(0, 1)])
    combine_step(1, 3, [(0, 0)])
    combine_step(1, 2)
    combine_step(1, 1)
    combine_step(0, 2)
    for h in range(2):
        for copy in sums(1, 1, h):
            copy.wait_recv()
    swap[0] = (acc1[32:, :] + q1[0, 32:].astype(F32) + q1[4, 32:].astype(F32)).astype(BF16)
    swap_out.start()
    acc1[:32, :] = acc1[:32, :] + q1[0, :32].astype(F32) + q1[4, :32].astype(F32)
    combine_step(0, 1)
    swap_out.wait_recv()
    out[1] = (acc1[:32, :] + swap[1].astype(F32)).astype(BF16)
    for h in range(2):
        cols = pl.ds(h * half, half)
        for copy in sums(0, 1, h):
            copy.wait_recv()
        out[0, :, cols] = (acc0[:, cols] + q0[0, :, cols].astype(F32) + q0[4, :, cols].astype(F32)).astype(BF16)

    for copy in pushes + swap_in + [swap_out]:
        copy.wait_send()
    for b in range(2):
        for k in range(1, 5):
            for c in range(2):
                for copy in [ring(b, k, way, c) for way in ways(k, c)] + sums(b, k, c):
                    copy.wait_send()
    for b in range(2):
        for j in range(PAIRS):
            for part in range(parts(b, j)):
                for copy in dispatch_copies(b, j, part)[0] + return_copies(b, j, part)[0]:
                    copy.wait_send()


def body(tokens, routing, route_gate, place_old, place_new, gate_proj, up_proj, down_proj):
    batches, rows, width = tokens.shape
    ff = gate_proj.shape[3]

    slots = PAIRS * PLANE * UNIT
    wide = width + META
    vm = pltpu.VMEM
    dma = pltpu.SemaphoreType.DMA
    anywhere = pl.BlockSpec(memory_space=pl.ANY)
    local = pl.BlockSpec(memory_space=pltpu.VMEM)
    return pl.pallas_call(
        kernel,
        out_shape=jax.ShapeDtypeStruct((batches, rows, width), BF16),
        in_specs=[anywhere] + [local] * 4 + [anywhere] * 3,
        out_specs=local,
        scratch_shapes=[
            vm((2, width, ff), BF16),
            vm((2, width, ff), BF16),
            vm((2, ff, width), BF16),
            vm((PAIRS, 2 * rows, wide), BF16),
            vm((PAIRS, 4 * rows, wide), BF16),
            vm((slots, width), BF16),
            vm((slots, width), BF16),
            vm((slots, width), BF16),
            vm((slots, width), BF16),
            vm((slots, width), BF16),
            vm((slots, width), BF16),
            vm((9, rows, width), BF16),
            vm((9, 2 * rows, width), BF16),
            vm((PAIRS, 4 * rows, 128), BF16),
            vm((PAIRS, 8 * rows, 128), BF16),
            vm((rows, width), F32),
            vm((2 * rows, width), F32),
            vm((256, 2 * ff), BF16),
            vm((META, 384), BF16),
            vm((2, rows, width), BF16),
            vm((rows, META), BF16),
            dma((3,)),
            dma((3,)),
            dma((3,)),
            dma((2,)),
            dma((3,)),
            dma((3,)),
            dma((2, 4, 2, 2)),
            dma((2, 4, 2, 2)),
            dma((2, PAIRS, 14)),
            dma((2, PAIRS, 14)),
            dma((2, PAIRS, 2)),
            dma((2, PAIRS, 14)),
            dma((2, PAIRS, 14)),
            dma((2, PAIRS, 2)),
            dma((2, 4, 2, 2)),
            dma((2, 4, 2, 2)),
        ],
        compiler_params=pltpu.CompilerParams(
            collective_id=0, has_side_effects=True, vmem_limit_bytes=62 * MIB
        ),
        name="expert_layer",
    )(
        tokens,
        jnp.swapaxes(routing, 1, 2),
        jnp.swapaxes(route_gate, 1, 2),
        place_old,
        place_new,
        gate_proj[0, 0],
        up_proj[0, 0],
        down_proj[0, 0],
    )


def solution(mesh):
    return jax.shard_map(
        body,
        mesh=mesh,
        in_specs=(
            P(None, ("rep", "ep"), None),
            P(None, ("rep", "ep"), None),
            P(None, ("rep", "ep"), None),
            P(),
            P(),
            P("rep", "ep", None, None),
            P("rep", "ep", None, None),
            P("rep", "ep", None, None),
        ),
        out_specs=P(None, ("rep", "ep"), None),
        check_vma=False,
    )
```

```python
import jax
import jax.numpy as jnp
from jax import lax
from jax.experimental import pallas as pl
from jax.experimental.pallas import tpu as pltpu
from jax.sharding import PartitionSpec as P

CAP = 8
BF16 = jnp.bfloat16
F32 = jnp.float32
NY, NZ, NX = 4, 8, 2
PLANE = NY * NX
PAIRS = 4
UNIT = 2 * CAP
META = 256
MESH = pl.DeviceIdType.MESH
MIB = 1 << 20


def kernel(
    tokens, routing, route_gate, place_old, place_new, gate_hbm, up_hbm, down_hbm, out,
    wg, wu, wd, g0, g1, s0, s1, r0, r1, t0, t1, q0, q1, w0, w1, acc0, acc1, hid, sel, swap, theirs,
    load_sem, wsend, wrecv, own_sem, xsend, xrecv,
    gsend, grecv, dsend, drecv, dloc, csend, crecv, cloc, rsend, rrecv,
):
    width = out.shape[2]
    wide = width + META
    half = width // 2
    tile = 512
    rows_of = (32, 64)
    block = PLANE * UNIT
    rep = lax.axis_index("rep")
    ep = lax.axis_index("ep")
    core = lax.rem(ep, 2)
    x = lax.rem(lax.div(ep, 2), NX)
    z = lax.rem(lax.div(ep, 2 * NX), NZ)
    y = lax.div(ep, 2 * NX * NZ)
    here = y * NX + x
    def at(yy, zz, xx):
        return (rep, ((yy * NZ + zz) * NX + xx) * 2 + core)

    right = at(y, lax.rem(z + 1, NZ), x)
    left = at(y, lax.rem(z + NZ - 1, NZ), x)
    other_rep = (1 - rep, ep)
    other_core = (rep, ep + 1 - 2 * core)
    plane = []
    for d in (1, 2, 6, 3, 7, 4, 5):
        yy, xx = lax.rem(y + d // NX, NY), lax.rem(x + d % NX, NX)
        plane.append((yy * NX + xx, at(yy, z, xx)))

    barrier = pltpu.get_barrier_semaphore()
    partners = [right, left, other_rep, other_core] + [dev for _, dev in plane]
    for dev in partners:
        pl.semaphore_signal(barrier, inc=1, device_id=dev, device_id_type=MESH)
    mine = pl.ds(0, 32)
    own = [
        pltpu.make_async_copy(tokens.at[b], g.at[3, mine, pl.ds(META, width)], own_sem.at[b])
        for b, g in enumerate((g0, g1))
    ]
    loads = [
        pltpu.make_async_copy(src, dst.at[0], load_sem.at[i])
        for i, (src, dst) in enumerate(((gate_hbm, wg), (up_hbm, wu), (down_hbm, wd)))
    ]
    for copy in own + loads:
        copy.start()

    first = rep == 0
    old = jnp.concatenate([place_old[...], place_old[...]], axis=1)
    new = jnp.concatenate([place_new[...], place_new[...]], axis=1)
    old_here = jnp.where(first, old[0:1], old[1:2])
    old_there = jnp.where(first, old[1:2], old[0:1])
    moved_here = old_here != jnp.where(first, new[0:1], new[1:2])
    moved_there = old_there != jnp.where(first, new[1:2], new[0:1])
    before = (
        lax.broadcasted_iota(jnp.int32, (32, 32), 0) > lax.broadcasted_iota(jnp.int32, (32, 32), 1)
    ).astype(F32)
    lower = lax.broadcasted_iota(jnp.int32, (32, 128), 1) < 64

    def describe(b, layout, served, ref):
        chosen, gates = routing[b].T, route_gate[b].T
        weight = jnp.zeros((32, 128), F32)
        named = jnp.zeros((32, 128), F32)
        for k in range(routing.shape[1]):
            hit = (chosen[:, k : k + 1] == layout) & served
            weight = weight + jnp.where(hit, gates[:, k : k + 1], 0.0)
            named = named + jnp.where(hit, 1.0, 0.0)
        rank = jnp.dot(before.astype(BF16), named.astype(BF16), preferred_element_type=F32)
        rank = jnp.where(named > 0.5, rank, -1.0)
        high = weight.astype(BF16).astype(F32)
        ref[:, :128] = jnp.where(lower, rank, high).astype(BF16)
        ref[:, 128:] = jnp.where(lower, weight - high, 0.0).astype(BF16)

    lanes = pl.ds(0, META)
    describe(0, old_here, old_here >= 0, g0.at[3, mine, lanes])
    describe(1, old_here, ~moved_here, g1.at[3, mine, lanes])
    describe(1, old_there, moved_there, theirs)
    pl.semaphore_wait(barrier, len(partners))

    def remote(src, dst, send, recv, dev):
        return pltpu.make_async_remote_copy(
            src_ref=src, dst_ref=dst, send_sem=send, recv_sem=recv, device_id=dev, device_id_type=MESH
        )

    def unit(p, j, count=UNIT):
        return pl.ds(pl.multiple_of(j * block + p * UNIT, UNIT), count)

    G, S, R, T, Q, W, ACC = (g0, g1), (s0, s1), (r0, r1), (t0, t1), (q0, q1), (w0, w1), (acc0, acc1)

    def ways(k, c):
        return (0, 1) if k < 4 else (c,)

    def ring(b, k, way, c):
        g, n = G[b], rows_of[b]
        cols = pl.ds(META + half, half) if c else pl.ds(0, META + half)
        src = g.at[3, pl.ds(0, n), cols] if k == 1 else g.at[k - 2, pl.ds(way * n, n), cols]
        dst = g.at[k - 1, pl.ds((way if k < 4 else 1) * n, n), cols]
        sems = (gsend.at[b, k - 1, way, c], grecv.at[b, k - 1, way, c])
        return remote(src, dst, *sems, left if way else right)

    def ring_start(b, c):
        for way in ways(1, c):
            ring(b, 1, way, c).start()

    def gather_chunk(b, k, c):
        for way in ways(k, c):
            ring(b, k, way, c).wait_recv()
            if k < 4 and way in ways(k + 1, c):
                ring(b, k + 1, way, c).start()

    def gather_step(b, k):
        gather_chunk(b, k, 0)
        gather_chunk(b, k, 1)

    def parts(b, j):
        return 2 if (b, j) == (0, 0) else 1

    def exchange(src, dst, sems, b, j, part):
        send, recv, loc = sems
        cols = pl.ds(part * half, half) if parts(b, j) == 2 else pl.ds(0, width)
        to = dst.at[unit(here, j), cols]
        remotes = [
            remote(src.at[unit(p, j), cols], to, send.at[b, j, 7 * part + d], recv.at[b, j, 7 * part + d], dev)
            for d, (p, dev) in enumerate(plane)
        ]
        return remotes, pltpu.make_async_copy(src.at[unit(here, j), cols], to, loc.at[b, j, part])

    def dispatch_copies(b, j, part):
        return exchange(S[b], R[b], (dsend, drecv, dloc), b, j, part)

    def begin(copies):
        remotes, local = copies
        for copy in remotes:
            copy.start()
        local.start()

    def landed(copies):
        remotes, local = copies
        for copy in remotes:
            copy.wait_recv()
        local.wait()

    def choose(b, j):
        g, w, n = G[b], W[b], rows_of[b]
        meta = jnp.dot(g[j, :, :META], sel[...], preferred_element_type=F32)
        lane = lax.broadcasted_iota(jnp.int32, (2 * n, 128), 1)
        row = lax.broadcasted_iota(jnp.int32, (2 * n, 128), 0)
        fits = (meta[:, :128] == (lane & 7).astype(F32)) & (((lane >> 3) & 1) == (row >= n).astype(jnp.int32))
        w[j, : 2 * n] = jnp.where(fits, meta[:, 128:256], 0.0).astype(BF16)
        w[j, 2 * n :] = jnp.where(fits, meta[:, 256:], 0.0).astype(BF16)
        return jnp.where(fits, 1.0, 0.0).T.astype(BF16)

    def pack(b, j, part, pick):
        g, s = G[b], S[b]
        step = tile // parts(b, j)

        @pl.loop(0, width // tile)
        def _(i):
            at_col = part * half + i * step
            s[pl.ds(j * block, block), pl.ds(pl.multiple_of(at_col, 256), step)] = jnp.dot(
                pick, g[j, :, pl.ds(pl.multiple_of(META + at_col, 256), step)], preferred_element_type=F32
            ).astype(BF16)

        begin(dispatch_copies(b, j, part))

    def dispatch_wait(b, j):
        for part in range(parts(b, j)):
            landed(dispatch_copies(b, j, part))

    def ffn(b, m):
        rows = pl.ds(m * 256, 256)
        r = R[b]

        @pl.loop(0, 4)
        def _(i):
            h = lax.div(i, 2)
            cols = pl.ds(pl.multiple_of(lax.rem(i, 2) * 256, 256), 256)
            gate = jnp.dot(r[rows, :], wg[h, :, cols], preferred_element_type=F32)
            up = jnp.dot(r[rows, :], wu[h, :, cols], preferred_element_type=F32)
            hid[:, pl.ds(pl.multiple_of(i * 256, 256), 256)] = (jax.nn.silu(gate) * up).astype(BF16)

        @pl.loop(0, width // tile)
        def _(i):
            cols = pl.ds(pl.multiple_of(i * tile, tile), tile)
            down = jnp.dot(hid[:, :512], wd[0, :, cols], preferred_element_type=F32)
            down = down + jnp.dot(hid[:, 512:], wd[1, :, cols], preferred_element_type=F32)
            r[rows, cols] = down.astype(BF16)

    def return_copies(b, j, part):
        return exchange(R[b], T[b], (csend, crecv, cloc), b, j, part)

    def give_back(b, j):
        for part in range(parts(b, j)):
            begin(return_copies(b, j, part))

    def sums(b, k, h):
        q = Q[b]
        cols = pl.ds(h * half, half)
        copies = []
        for way in ways(k, h):
            src = q.at[8, :, cols] if k == 4 else q.at[4 * way + k, :, cols]
            dst = q.at[4 * way + k - 1, :, cols]
            sems = (rsend.at[b, k - 1, way, h], rrecv.at[b, k - 1, way, h])
            copies.append(remote(src, dst, *sems, left if way else right))
        return copies

    def combine_step(b, k, then=()):
        q, t, w, n = Q[b], T[b], W[b], rows_of[b]
        j = k - 1
        landed(return_copies(b, j, 0))
        for later in then:
            give_back(*later)
        for h in range(2):
            if h and parts(b, j) == 2:
                landed(return_copies(b, j, 1))
            if k < 4:
                for copy in sums(b, k + 1, h):
                    copy.wait_recv()

            @pl.loop(0, half // 256)
            def _(i):
                cols = pl.ds(pl.multiple_of(h * half + i * 256, 256), 256)
                both = jnp.dot(w[j], t[pl.ds(j * block, block), cols], preferred_element_type=F32)
                part = both[: 2 * n] + both[2 * n :]
                if k == 4:
                    ACC[b][:, cols] = part[:n]
                    q[8, :, cols] = part[n:].astype(BF16)
                else:
                    to_left, to_right = part[:n], part[n:]
                    if k < 3 or h == 0:
                        to_right = to_right + q[k, :, cols].astype(F32)
                    if k < 3 or h == 1:
                        to_left = to_left + q[4 + k, :, cols].astype(F32)
                    q[k, :, cols] = to_right.astype(BF16)
                    q[4 + k, :, cols] = to_left.astype(BF16)

            for copy in sums(b, k, h):
                copy.start()

    swap_in = [
        remote(tokens.at[1], g1.at[3, pl.ds(32, 32), pl.ds(META, width)], xsend.at[0], xrecv.at[0], other_rep),
        remote(theirs, g1.at[3, pl.ds(32, 32), lanes], xsend.at[1], xrecv.at[1], other_rep),
    ]
    swap_out = remote(swap.at[0], swap.at[1], xsend.at[2], xrecv.at[2], other_rep)
    for copy in own:
        copy.wait()
    ring_start(0, 0)
    ring_start(0, 1)
    for copy in swap_in:
        copy.start()
    pushes = [
        remote(src, dst.at[1], wsend.at[i], wrecv.at[i], other_core)
        for i, (src, dst) in enumerate(((gate_hbm, wg), (up_hbm, wu), (down_hbm, wd)))
    ]
    for copy in pushes:
        copy.start()

    lane_of = lax.broadcasted_iota(jnp.int32, (META, 384), 0)
    slot = lax.broadcasted_iota(jnp.int32, (META, 384), 1)
    place = lane_of & 63
    chosen = ((lane_of >> 6) == (slot >> 7)) & (((place >> 1) & (NZ - 1)) == z)
    chosen = chosen & (NX * (place >> 4) + (place & 1) == ((slot & 127) >> 4))
    sel[...] = jnp.where(chosen, 1.0, 0.0).astype(BF16)

    gather_chunk(0, 1, 0)
    pick = choose(0, 0)
    pack(0, 0, 0, pick)
    gather_chunk(0, 1, 1)
    pack(0, 0, 1, pick)
    for k in range(2, 5):
        gather_step(0, k)
        if k == 2:
            for copy in swap_in:
                copy.wait_recv()
            ring_start(1, 0)
            ring_start(1, 1)
        pack(0, k - 1, 0, choose(0, k - 1))

    gather_step(1, 1)
    pack(1, 0, 0, choose(1, 0))
    for copy in loads:
        copy.wait()
    for copy in pushes:
        copy.wait_recv()
    dispatch_wait(0, 0)
    dispatch_wait(0, 1)
    ffn(0, 0)
    gather_step(1, 2)
    pack(1, 1, 0, choose(1, 1))
    gather_step(1, 3)
    pack(1, 2, 0, choose(1, 2))
    gather_step(1, 4)
    pack(1, 3, 0, choose(1, 3))
    dispatch_wait(0, 2)
    dispatch_wait(0, 3)
    ffn(0, 1)
    dispatch_wait(1, 0)
    dispatch_wait(1, 1)
    give_back(0, 3)
    ffn(1, 0)
    dispatch_wait(1, 2)
    give_back(0, 2)
    dispatch_wait(1, 3)
    ffn(1, 1)
    give_back(1, 3)
    give_back(1, 2)
    combine_step(0, 4, [(1, 1)])
    combine_step(0, 3, [(1, 0)])
    combine_step(1, 4, [(0, 1)])
    combine_step(1, 3, [(0, 0)])
    combine_step(1, 2)
    combine_step(1, 1)
    combine_step(0, 2)
    for h in range(2):
        for copy in sums(1, 1, h):
            copy.wait_recv()
    swap[0] = (acc1[32:, :] + q1[0, 32:].astype(F32) + q1[4, 32:].astype(F32)).astype(BF16)
    swap_out.start()
    acc1[:32, :] = acc1[:32, :] + q1[0, :32].astype(F32) + q1[4, :32].astype(F32)
    combine_step(0, 1)
    swap_out.wait_recv()
    out[1] = (acc1[:32, :] + swap[1].astype(F32)).astype(BF16)
    for h in range(2):
        cols = pl.ds(h * half, half)
        for copy in sums(0, 1, h):
            copy.wait_recv()
        out[0, :, cols] = (acc0[:, cols] + q0[0, :, cols].astype(F32) + q0[4, :, cols].astype(F32)).astype(BF16)

    for copy in pushes + swap_in + [swap_out]:
        copy.wait_send()
    for b in range(2):
        for k in range(1, 5):
            for c in range(2):
                for copy in [ring(b, k, way, c) for way in ways(k, c)] + sums(b, k, c):
                    copy.wait_send()
    for b in range(2):
        for j in range(PAIRS):
            for part in range(parts(b, j)):
                for copy in dispatch_copies(b, j, part)[0] + return_copies(b, j, part)[0]:
                    copy.wait_send()


def body(tokens, routing, route_gate, place_old, place_new, gate_proj, up_proj, down_proj):
    batches, rows, width = tokens.shape
    ff = gate_proj.shape[3]

    slots = PAIRS * PLANE * UNIT
    wide = width + META
    vm = pltpu.VMEM
    dma = pltpu.SemaphoreType.DMA
    anywhere = pl.BlockSpec(memory_space=pl.ANY)
    local = pl.BlockSpec(memory_space=pltpu.VMEM)
    return pl.pallas_call(
        kernel,
        out_shape=jax.ShapeDtypeStruct((batches, rows, width), BF16),
        in_specs=[anywhere] + [local] * 4 + [anywhere] * 3,
        out_specs=local,
        scratch_shapes=[
            vm((2, width, ff), BF16),
            vm((2, width, ff), BF16),
            vm((2, ff, width), BF16),
            vm((PAIRS, 2 * rows, wide), BF16),
            vm((PAIRS, 4 * rows, wide), BF16),
            vm((slots, width), BF16),
            vm((slots, width), BF16),
            vm((slots, width), BF16),
            vm((slots, width), BF16),
            vm((slots, width), BF16),
            vm((slots, width), BF16),
            vm((9, rows, width), BF16),
            vm((9, 2 * rows, width), BF16),
            vm((PAIRS, 4 * rows, 128), BF16),
            vm((PAIRS, 8 * rows, 128), BF16),
            vm((rows, width), F32),
            vm((2 * rows, width), F32),
            vm((256, 2 * ff), BF16),
            vm((META, 384), BF16),
            vm((2, rows, width), BF16),
            vm((rows, META), BF16),
            dma((3,)),
            dma((3,)),
            dma((3,)),
            dma((2,)),
            dma((3,)),
            dma((3,)),
            dma((2, 4, 2, 2)),
            dma((2, 4, 2, 2)),
            dma((2, PAIRS, 14)),
            dma((2, PAIRS, 14)),
            dma((2, PAIRS, 2)),
            dma((2, PAIRS, 14)),
            dma((2, PAIRS, 14)),
            dma((2, PAIRS, 2)),
            dma((2, 4, 2, 2)),
            dma((2, 4, 2, 2)),
        ],
        compiler_params=pltpu.CompilerParams(
            collective_id=0, has_side_effects=True, vmem_limit_bytes=62 * MIB
        ),
        name="expert_layer",
    )(
        tokens,
        jnp.swapaxes(routing, 1, 2),
        jnp.swapaxes(route_gate, 1, 2),
        place_old,
        place_new,
        gate_proj[0, 0],
        up_proj[0, 0],
        down_proj[0, 0],
    )


def solution(mesh):
    return jax.shard_map(
        body,
        mesh=mesh,
        in_specs=(
            P(None, ("rep", "ep"), None),
            P(None, ("rep", "ep"), None),
            P(None, ("rep", "ep"), None),
            P(),
            P(),
            P("rep", "ep", None, None),
            P("rep", "ep", None, None),
            P("rep", "ep", None, None),
        ),
        out_specs=P(None, ("rep", "ep"), None),
        check_vma=False,
    )
```
